128 devices in a mesh: pair: 16 (over y, x), ctr: 8 (over z, core).
Axes of the slice: x: 4, y: 4, z: 4, core: 2. Of those that a mesh axis runs over, the one named last changes fastest.
Arguments:
- amp_tiles: bfloat16 [32768, 9216], P(('pair', 'ctr')), may hold values from -6 to 6
- amp_rows: int32 [32768], P(('pair', 'ctr')), may hold values from 0 to 191, as said below
- amp_cols: int32 [32768], P(('pair', 'ctr')), may hold values from 0 to 191
- int_tiles: bfloat16 [8, 288, 9216], P('ctr', 'pair'), may hold values from -0.0625 to 0.0625
- int_rows: int32 [8, 288], P('ctr', 'pair'), may hold values from 0 to 191, as said below
- int_cols: int32 [8, 288], P('ctr', 'pair'), may hold values from 0 to 23
Outputs:
- cycle: bfloat16 [18432, 2304], P(('pair', 'ctr'))
The draws below stay inside these ranges and needn't reach their ends.
Inputs may be any that keep to these rules, and one draw needn't show every extreme that they name: Together with amp_cols, no position is named twice. A tile's owner is the device with pair index amp_rows // 12 and ctr index amp_cols // 24. Each device holds at most 4 tiles of one owner, exactly that many for some owners in every draw, and every device owns exactly 256 tiles. int_rows[g, t] lies in g * 2 * 12 to (g + 1) * 2 * 12 - 1; no pair (int_rows, int_cols) is named twice.
All inputs are finite; a program needn't handle non-finite values.
Results may differ from the reference program's by a relative error of at most 0.017.
Values may be sent and summed in bfloat16 or wider, within the bound.
No kernel may reach another device: no remote copies, remote signals or barrier semaphores. Data moves between devices by JAX's collectives and lax.ppermute only.
A program may use at most 192 MiB of HBM per device.

```python
import jax
import jax.numpy as jnp
from jax import lax

TILE = 96
VT = 12
OI_DEV = 1
OK_DEV = 2
OJ = 2
TA_DEV = 256
WT_DEV = 18
N_PAIR = 16
N_CTR = 8
DEVICES = 128


def amp_layout(key):
    key = jax.random.fold_in(key, 7)
    devices = N_PAIR * N_CTR
    rows_dev = OI_DEV * VT
    ctr_dev = OK_DEV * VT
    share = TA_DEV // devices
    eighth = devices // 8
    base = jnp.concatenate([jnp.full((eighth,), share, jnp.int32), jnp.full((eighth,), -share, jnp.int32), jnp.full((eighth,), share // 2, jnp.int32), jnp.full((eighth,), -(share // 2), jnp.int32), jnp.zeros((devices - 4 * eighth,), jnp.int32)])
    key_one, key_two, key_three = jax.random.split(key, 3)
    pattern = jax.random.permutation(key_one, base)
    source = jnp.arange(devices)[:, None]
    target = jnp.arange(devices)[None, :]
    counts = share + pattern[(target - source) % devices]
    before = jnp.cumsum(counts, axis=0) - counts
    ends = jnp.cumsum(counts, axis=1)
    slots = jnp.arange(TA_DEV)
    dest = jnp.sum((slots[None, :, None] >= ends[:, None, :]).astype(jnp.int32), axis=2)
    begin = jnp.take_along_axis(ends - counts, dest, axis=1)
    which = jnp.take_along_axis(before, dest, axis=1) + slots[None, :] - begin
    places = jax.vmap(lambda sub: jax.random.permutation(sub, rows_dev * ctr_dev))(jax.random.split(key_two, devices))[:, :TA_DEV]
    spots = places[dest, which]
    rows = dest // N_CTR * rows_dev + spots // ctr_dev
    cols = dest % N_CTR * ctr_dev + spots % ctr_dev
    order = jax.vmap(lambda sub: jax.random.permutation(sub, TA_DEV))(jax.random.split(key_three, devices))
    rows = jnp.take_along_axis(rows, order, axis=1).reshape(-1)
    cols = jnp.take_along_axis(cols, order, axis=1).reshape(-1)
    return (rows.astype(jnp.int32), cols.astype(jnp.int32))


def int_layout(key):
    key = jax.random.fold_in(key, 101)
    ctr_dev = OK_DEV * VT
    col_tiles = OJ * VT
    count = N_PAIR * WT_DEV
    places = jax.vmap(lambda sub: jax.random.permutation(sub, ctr_dev * col_tiles))(jax.random.split(key, N_CTR))[:, :count]
    groups = jnp.arange(N_CTR)[:, None]
    rows = groups * ctr_dev + places // col_tiles
    cols = places % col_tiles
    return (rows.astype(jnp.int32), cols.astype(jnp.int32))


def draw_amp_rows(key, part):
    rows, cols = amp_layout(key)
    return rows


def draw_amp_cols(key, part):
    rows, cols = amp_layout(key)
    return cols


def draw_int_rows(key, part):
    rows, cols = int_layout(key)
    return rows


def draw_int_cols(key, part):
    rows, cols = int_layout(key)
    return cols


def levels(rng, dims, cuts, least, top_value):
    factor_of, own = 1.0, jax.random.fold_in(rng, 6)
    for position, shards_of in cuts:
        heights = jnp.exp(jax.random.uniform(jax.random.fold_in(own, position), (shards_of,), jnp.float32, least / len(cuts), top_value / len(cuts)))
        factor_of = factor_of * jnp.repeat(heights, dims[position] // shards_of).reshape([-1 if axis == position else 1 for axis in range(len(dims))])
    return factor_of


def bell_draw(rng, extent, spread, bound, cuts=(), held_as=jnp.bfloat16):
    result = jax.random.normal(rng, extent, jnp.float32) * spread
    if len(cuts) > 0:
        result = levels(rng, extent, cuts, -0.22, 0.18) * result
    return jnp.clip(result, min=-bound, max=bound).astype(held_as)


def setup_inputs(seed: int = 0) -> dict:
    seeds = jax.random.split(jax.random.key(seed), 7)
    return {
        "amp_tiles": bell_draw(seeds[0], (DEVICES * TA_DEV, TILE * TILE), 1.0, 6.0, ((0, 128),)),
        "amp_rows": draw_amp_rows(jax.random.fold_in(seeds[6], 71), 0),
        "amp_cols": draw_amp_cols(jax.random.fold_in(seeds[6], 71), 0),
        "int_tiles": bell_draw(seeds[3], (N_CTR, N_PAIR * WT_DEV, TILE * TILE), (TA_DEV * N_CTR * TILE // (2 * OI_DEV * VT)) ** -0.5, 0.0625, ((0, 8), (1, 16))),
        "int_rows": draw_int_rows(jax.random.fold_in(seeds[6], 71), 0),
        "int_cols": draw_int_cols(jax.random.fold_in(seeds[6], 71), 0),
    }


def reference(amp_tiles, amp_rows, amp_cols, int_tiles, int_rows, int_cols):
    row_tiles = OI_DEV * N_PAIR * VT
    ctr_tiles = OK_DEV * VT
    col_tiles = OJ * VT
    tiles = amp_tiles.reshape(-1, TILE, TILE).astype(jnp.float32)
    total = jnp.zeros((row_tiles * TILE, col_tiles * TILE), jnp.float32)
    for group in range(N_CTR):
        local_cols = amp_cols - group * ctr_tiles
        inside = (local_cols >= 0) & (local_cols < ctr_tiles)
        slots = jnp.where(inside, local_cols, ctr_tiles).astype(jnp.int32)
        block = jnp.zeros((row_tiles, ctr_tiles, TILE, TILE), jnp.float32)
        block = block.at[amp_rows.astype(jnp.int32), slots].add(tiles, mode="drop")
        left = block.transpose(0, 2, 1, 3).reshape(row_tiles * TILE, ctr_tiles * TILE)
        weights = int_tiles[group].reshape(-1, TILE, TILE).astype(jnp.float32)
        grid = jnp.zeros((ctr_tiles, col_tiles, TILE, TILE), jnp.float32)
        grid = grid.at[(int_rows[group] - group * ctr_tiles).astype(jnp.int32), int_cols[group].astype(jnp.int32)].add(weights)
        right = grid.transpose(0, 2, 1, 3).reshape(ctr_tiles * TILE, col_tiles * TILE)
        partial_value = jnp.dot(left, right, preferred_element_type=jnp.float32).astype(jnp.bfloat16)
        partial_value = lax.optimization_barrier(partial_value)
        total = total + partial_value.astype(jnp.float32)
    return total.astype(jnp.bfloat16)
```

```python
import jax
import jax.numpy as jnp
from jax import lax
from jax.experimental import pallas as pl
from jax.experimental.pallas import tpu as pltpu
from jax.sharding import PartitionSpec as P

TILE = 96
VT = 12
KT = 24
JT = 24
FLAT = TILE * TILE
HALF = FLAT // 2
QUARTER = FLAT // 4
SLOTS = 4
LANES = 128
MIB = 2**20


def quad_unpack(v0, v1, v2, lane):
    return (v0, jnp.where(lane >= 96, v0, v1), jnp.where(lane >= 64, v1, v2), v2)


def turn(x, amount):
    amount = amount % LANES
    return x if amount == 0 else pltpu.roll(x, amount, 1)


def pack_kernel(land_ref, lab_ref, low_ref, high_ref, out_ref, first, second):
    step = pl.program_id(0)
    rows = first.shape[0]

    @pl.when(step == 0)
    def _():
        row = lax.broadcasted_iota(jnp.int32, first.shape, 0)
        land = jnp.broadcast_to(land_ref[...], first.shape)
        first[...] = jnp.where(row == land, 1.0, 0.0).astype(jnp.bfloat16)
        second[...] = jnp.where((row ^ SLOTS) == land, 1.0, 0.0).astype(jnp.bfloat16)

    def spread(low, high):
        a = jnp.dot(first[...], low, preferred_element_type=jnp.float32)
        b = jnp.dot(second[...], high, preferred_element_type=jnp.float32)
        n = a.shape[1]
        a = a.reshape(rows // 8, 1, 8, n)
        b = b.reshape(rows // 8, 1, 8, n)
        top = lax.broadcasted_iota(jnp.int32, a.shape, 2) < SLOTS
        both = jnp.concatenate([jnp.where(top, a, b), jnp.where(top, b, a)], axis=1)
        return both.reshape(rows * 2, n).astype(jnp.bfloat16)

    @pl.when(step < pl.num_programs(0) - 1)
    def _():
        out_ref[...] = spread(low_ref[...], high_ref[...])

    @pl.when(step == pl.num_programs(0) - 1)
    def _():
        out_ref[:, :LANES] = spread(lab_ref[...], lab_ref[...])


def pack(land, labels, tiles, devices):
    held = tiles.shape[0]
    block = 512
    steps = HALF // block
    return pl.pallas_call(
        pack_kernel,
        grid=(steps + 1,),
        out_shape=jax.ShapeDtypeStruct((devices * 2 * SLOTS, HALF + LANES), jnp.bfloat16),
        in_specs=[
            pl.BlockSpec((1, held), lambda s: (0, 0)),
            pl.BlockSpec((held, LANES), lambda s: (0, 0)),
            pl.BlockSpec((held, block), lambda s: (0, jnp.minimum(s, steps - 1))),
            pl.BlockSpec((held, block), lambda s: (0, steps + jnp.minimum(s, steps - 1))),
        ],
        out_specs=pl.BlockSpec((devices * 2 * SLOTS, block), lambda s: (0, s)),
        scratch_shapes=[pltpu.VMEM((devices * SLOTS, held), jnp.bfloat16)] * 2,
        compiler_params=pltpu.CompilerParams(vmem_limit_bytes=40 * MIB),
        name="pack",
    )(land, labels, tiles, tiles)


def label_rows(lab):
    unit = (
        lax.broadcasted_iota(jnp.int32, (8, LANES), 0)
        == lax.broadcasted_iota(jnp.int32, (8, LANES), 1)
    )
    return lax.dot_general(
        jnp.where(unit, 1.0, 0.0).astype(jnp.bfloat16),
        lab,
        (((1,), (1,)), ((), ())),
        preferred_element_type=jnp.float32,
    )


def integral_kernel(lab_ref, tiles_ref, out_ref, spread):
    quad = pl.program_id(0)
    labels = label_rows(lab_ref[...])
    cell = (labels[0:1] * 4 + labels[1:2] * (4 * KT) + labels[2:3]).astype(jnp.int32)
    shape = (4 * 4 * KT, lab_ref.shape[0])
    row = lax.broadcasted_iota(jnp.int32, shape, 0) + quad * (4 * 4 * KT)
    choose = jnp.where(row == jnp.broadcast_to(cell, shape), 1.0, 0.0).astype(jnp.bfloat16)
    for group in range(QUARTER // 384):
        block = jnp.dot(
            choose, tiles_ref[:, group * 384 : (group + 1) * 384], preferred_element_type=jnp.float32
        )
        lane = lax.broadcasted_iota(jnp.int32, (shape[0], LANES), 1)
        pieces = quad_unpack(block[:, :128], block[:, 128:256], block[:, 256:], lane)
        for a in range(4):
            for b in range(4):
                spread[b, pl.ds(group * 4 + a, 4 * KT, stride=24), :] = turn(
                    pieces[a][b * 96 : (b + 1) * 96], 32 * (a - b)
                )
    for part in range(KT):
        at = slice(part * 96, (part + 1) * 96)
        w = [spread[b, at, :] for b in range(4)]
        lane = lax.broadcasted_iota(jnp.int32, (96, LANES), 1)
        out_ref[at, 0:128] = jnp.where(lane < 96, w[0], w[1]).astype(jnp.bfloat16)
        out_ref[at, 128:256] = jnp.where(lane < 64, w[1], w[2]).astype(jnp.bfloat16)
        out_ref[at, 256:384] = jnp.where(lane < 32, w[2], w[3]).astype(jnp.bfloat16)


def place_integrals(gathered):
    rows = gathered.shape[0]
    return pl.pallas_call(
        integral_kernel,
        grid=(JT // 4,),
        out_shape=jax.ShapeDtypeStruct((KT * TILE, JT * TILE), jnp.bfloat16),
        in_specs=[
            pl.BlockSpec((rows, LANES), lambda s: (0, QUARTER // LANES)),
            pl.BlockSpec((rows, QUARTER), lambda s: (0, 0)),
        ],
        out_specs=pl.BlockSpec((KT * TILE, 4 * TILE), lambda s: (0, s)),
        scratch_shapes=[pltpu.VMEM((4, KT * TILE, LANES), jnp.float32)],
        compiler_params=pltpu.CompilerParams(vmem_limit_bytes=40 * MIB),
        name="integrals",
    )(gathered, gathered)


def product_kernel(odd_ref, lab_ref, low_ref, high_ref, b_ref, out_ref, choose, amp, total):
    step = pl.program_id(0)
    groups = QUARTER // 384

    @pl.when(step == 0)
    def _():
        labels = label_rows(lab_ref[...])
        column = lax.broadcasted_iota(jnp.int32, (1, lab_ref.shape[0]), 1)
        second = ((column & SLOTS) // SLOTS) ^ odd_ref[0]
        k = labels[0:1].astype(jnp.int32) - 1
        i = labels[1:2].astype(jnp.int32)
        cell = k * (2 * VT) + second * VT + i
        row = lax.broadcasted_iota(jnp.int32, choose.shape, 0)
        choose[...] = jnp.where(row == jnp.broadcast_to(cell, choose.shape), 1.0, 0.0).astype(
            jnp.bfloat16
        )

    @pl.when(step < groups)
    def _():
        low = jnp.dot(choose[...], low_ref[...], preferred_element_type=jnp.float32)
        high = jnp.dot(choose[...], high_ref[...], preferred_element_type=jnp.float32)
        lane = lax.broadcasted_iota(jnp.int32, (48, LANES), 1)
        for quad in range(KT // 4):
            pieces = []
            for b in range(4):
                at = slice((quad * 4 + b) * 24, (quad * 4 + b + 1) * 24)
                both = jnp.concatenate([low[at], high[at]], axis=0)
                pieces.append(quad_unpack(both[:, :128], both[:, 128:256], both[:, 256:], lane))
            for a in range(4):
                w = [turn(pieces[b][a], 32 * (a - b)) for b in range(4)]
                at = pl.ds(pl.multiple_of((step * 4 + a) * 48, 16), 48)
                base = quad * 384
                amp[at, base : base + 128] = jnp.where(lane < 96, w[0], w[1]).astype(jnp.bfloat16)
                amp[at, base + 128 : base + 256] = jnp.where(lane < 64, w[1], w[2]).astype(jnp.bfloat16)
                amp[at, base + 256 : base + 384] = jnp.where(lane < 32, w[2], w[3]).astype(jnp.bfloat16)

    @pl.when(step >= groups)
    def _():
        value = jnp.dot(amp[...], b_ref[...], preferred_element_type=jnp.float32)
        for part in range(total.shape[0]):
            lanes = slice(part * LANES, (part + 1) * LANES)
            total[part] = value[:, lanes]
            for i in range(VT):
                for h in range(2):
                    x = h * VT + i
                    rows = [total[part, pl.ds(x + 24 * q, 24, stride=48), :] for q in range(2)]
                    at = i * 96 + h * 48
                    out_ref[at : at + 48, lanes] = jnp.concatenate(rows, axis=0).astype(jnp.bfloat16)


def product(odd, arrived, integrals):
    groups = QUARTER // 384
    block = 256
    steps = integrals.shape[1] // block
    rows = arrived.shape[0]
    early = lambda s: jnp.minimum(s, groups - 1)
    late = lambda s: jnp.maximum(s - groups, 0)
    return pl.pallas_call(
        product_kernel,
        grid=(groups + steps,),
        out_shape=jax.ShapeDtypeStruct((VT * TILE, JT * TILE), jnp.bfloat16),
        in_specs=[
            pl.BlockSpec(memory_space=pltpu.SMEM),
            pl.BlockSpec((rows, LANES), lambda s: (0, HALF // LANES)),
            pl.BlockSpec((rows, 384), lambda s: (0, early(s))),
            pl.BlockSpec((rows, 384), lambda s: (0, groups + early(s))),
            pl.BlockSpec((KT * TILE, block), lambda s: (0, late(s))),
        ],
        out_specs=pl.BlockSpec((VT * TILE, block), lambda s: (0, late(s))),
        scratch_shapes=[
            pltpu.VMEM((2 * VT * KT, rows), jnp.bfloat16),
            pltpu.VMEM((VT * TILE, KT * TILE), jnp.bfloat16),
            pltpu.VMEM((block // LANES, VT * TILE, LANES), jnp.float32),
        ],
        compiler_params=pltpu.CompilerParams(vmem_limit_bytes=48 * MIB),
        name="product",
    )(odd, arrived, arrived, arrived, integrals)


def lanes_of(columns):
    stacked = jnp.stack(columns, axis=1).astype(jnp.bfloat16)
    return jnp.pad(stacked, ((0, 0), (0, LANES - stacked.shape[1])))


def on_device(amp_tiles, amp_rows, amp_cols, int_tiles, int_rows, int_cols):
    ctr_count = lax.axis_size("ctr")
    devices = lax.axis_size("pair") * ctr_count
    held = amp_tiles.shape[0]
    quarters = int_tiles[0].reshape(-1, 4, QUARTER).transpose(1, 0, 2).reshape(-1, QUARTER)
    four = jnp.repeat(jnp.arange(4, dtype=jnp.int32), int_rows.shape[1])
    int_labels = lanes_of([jnp.tile(int_rows[0] % KT, 4), jnp.tile(int_cols[0], 4), four])
    piece = jnp.concatenate([quarters, int_labels], axis=1)
    gathered = lax.all_gather(piece, "pair", axis=0, tiled=True)
    target = amp_rows // VT * ctr_count + amp_cols // KT
    order = jnp.arange(held, dtype=jnp.int32)
    earlier = (target[:, None] == target[None, :]) & (order[:, None] < order[None, :])
    land = target * SLOTS + jnp.sum(earlier.astype(jnp.int32), axis=0)
    labels = lanes_of([amp_cols % KT + 1, amp_rows % VT])
    outgoing = pack(land[None, :], labels, amp_tiles, devices)
    arrived = lax.all_to_all(outgoing, ("pair", "ctr"), split_axis=0, concat_axis=0, tiled=True)
    integrals = place_integrals(gathered)
    odd = (lax.axis_index("ctr") % 2).astype(jnp.int32).reshape(1)
    partial_value = product(odd, arrived, integrals)
    return lax.psum_scatter(partial_value, "ctr", scatter_dimension=0, tiled=True)


def solution(mesh):
    placed = (
        P(("pair", "ctr"), None),
        P(("pair", "ctr")),
        P(("pair", "ctr")),
        P("ctr", "pair", None),
        P("ctr", "pair"),
        P("ctr", "pair"),
    )
    return jax.shard_map(
        on_device, mesh=mesh, in_specs=placed, out_specs=P(("pair", "ctr"), None), check_vma=False
    )
```

```python
import jax
import jax.numpy as jnp
from jax import lax
from jax.experimental import pallas as pl
from jax.experimental.pallas import tpu as pltpu
from jax.sharding import PartitionSpec as P

TILE = 96
VT = 12
KT = 24
JT = 24
FLAT = TILE * TILE
HALF = FLAT // 2
QUARTER = FLAT // 4
SLOTS = 4
LANES = 128
MIB = 2**20


def quad_unpack(v0, v1, v2, lane):
    return (v0, jnp.where(lane >= 96, v0, v1), jnp.where(lane >= 64, v1, v2), v2)


def turn(x, amount):
    amount = amount % LANES
    return x if amount == 0 else pltpu.roll(x, amount, 1)


def pack_kernel(land_ref, lab_ref, low_ref, high_ref, out_ref, first, second):
    step = pl.program_id(0)
    rows = first.shape[0]

    @pl.when(step == 0)
    def _():
        row = lax.broadcasted_iota(jnp.int32, first.shape, 0)
        land = jnp.broadcast_to(land_ref[...], first.shape)
        first[...] = jnp.where(row == land, 1.0, 0.0).astype(jnp.bfloat16)
        second[...] = jnp.where((row ^ SLOTS) == land, 1.0, 0.0).astype(jnp.bfloat16)

    def spread(low, high):
        a = jnp.dot(first[...], low, preferred_element_type=jnp.float32)
        b = jnp.dot(second[...], high, preferred_element_type=jnp.float32)
        n = a.shape[1]
        a = a.reshape(rows // 8, 1, 8, n)
        b = b.reshape(rows // 8, 1, 8, n)
        top = lax.broadcasted_iota(jnp.int32, a.shape, 2) < SLOTS
        both = jnp.concatenate([jnp.where(top, a, b), jnp.where(top, b, a)], axis=1)
        return both.reshape(rows * 2, n).astype(jnp.bfloat16)

    @pl.when(step < pl.num_programs(0) - 1)
    def _():
        out_ref[...] = spread(low_ref[...], high_ref[...])

    @pl.when(step == pl.num_programs(0) - 1)
    def _():
        out_ref[:, :LANES] = spread(lab_ref[...], lab_ref[...])


def pack(land, labels, tiles, devices):
    held = tiles.shape[0]
    block = 512
    steps = HALF // block
    return pl.pallas_call(
        pack_kernel,
        grid=(steps + 1,),
        out_shape=jax.ShapeDtypeStruct((devices * 2 * SLOTS, HALF + LANES), jnp.bfloat16),
        in_specs=[
            pl.BlockSpec((1, held), lambda s: (0, 0)),
            pl.BlockSpec((held, LANES), lambda s: (0, 0)),
            pl.BlockSpec((held, block), lambda s: (0, jnp.minimum(s, steps - 1))),
            pl.BlockSpec((held, block), lambda s: (0, steps + jnp.minimum(s, steps - 1))),
        ],
        out_specs=pl.BlockSpec((devices * 2 * SLOTS, block), lambda s: (0, s)),
        scratch_shapes=[pltpu.VMEM((devices * SLOTS, held), jnp.bfloat16)] * 2,
        compiler_params=pltpu.CompilerParams(vmem_limit_bytes=56 * MIB),
        name="pack",
    )(land, labels, tiles, tiles)


def label_rows(lab):
    unit = (
        lax.broadcasted_iota(jnp.int32, (8, LANES), 0)
        == lax.broadcasted_iota(jnp.int32, (8, LANES), 1)
    )
    return lax.dot_general(
        jnp.where(unit, 1.0, 0.0).astype(jnp.bfloat16),
        lab,
        (((1,), (1,)), ((), ())),
        preferred_element_type=jnp.float32,
    )


def integral_kernel(k_ref, j_ref, tiles_ref, out_ref, spread):
    step = pl.program_id(0)
    held = (tiles_ref.shape[1] - 1) // TILE

    @pl.when(step == 0)
    def _():
        def clear(at, carry):
            spread[at] = jnp.zeros(spread.shape[1:], spread.dtype)
            return carry

        lax.fori_loop(0, JT, clear, 0)
        lane = lax.broadcasted_iota(jnp.int32, (TILE, LANES), 1)

        def source(at, carry):
            rows = pl.ds(pl.multiple_of(at * TILE, TILE), TILE)
            for quad in range(-(-held // 4)):
                v = [
                    tiles_ref[rows, (quad * 3 + n) * LANES : (quad * 3 + n + 1) * LANES].astype(jnp.float32)
                    if (quad * 3 + n) * LANES < tiles_ref.shape[1]
                    else None
                    for n in range(3)
                ]
                v = [v[0] if x is None else x for x in v]
                pieces = quad_unpack(*v, lane)
                for a in range(min(4, held - quad * 4)):
                    k = k_ref[at * held + quad * 4 + a]
                    j = j_ref[at * held + quad * 4 + a]
                    amount = (32 * a + 96 * (j % 4)) % LANES
                    spread[j, pl.ds(pl.multiple_of(k * TILE, TILE), TILE), :] = pltpu.roll(
                        pieces[a], amount, 1
                    ).astype(jnp.bfloat16)
            return carry

        lax.fori_loop(0, tiles_ref.shape[0] // TILE, source, 0)

    size = 256

    def join(at, carry):
        rows = pl.ds(pl.multiple_of(at * size, size), size)
        lane = lax.broadcasted_iota(jnp.int32, (size, LANES), 1)
        w = [spread[step * 4 + b, rows, :].astype(jnp.float32) for b in range(4)]
        out_ref[rows, 0:128] = jnp.where(lane < 96, w[0], w[1]).astype(jnp.bfloat16)
        out_ref[rows, 128:256] = jnp.where(lane < 64, w[1], w[2]).astype(jnp.bfloat16)
        out_ref[rows, 256:384] = jnp.where(lane < 32, w[2], w[3]).astype(jnp.bfloat16)
        return carry

    lax.fori_loop(0, KT * TILE // size, join, 0)


def place_integrals(k, j, gathered):
    return pl.pallas_call(
        integral_kernel,
        grid=(JT // 4,),
        out_shape=jax.ShapeDtypeStruct((KT * TILE, JT * TILE), jnp.bfloat16),
        in_specs=[
            pl.BlockSpec(memory_space=pltpu.SMEM),
            pl.BlockSpec(memory_space=pltpu.SMEM),
            pl.BlockSpec(gathered.shape, lambda s: (0, 0)),
        ],
        out_specs=pl.BlockSpec((KT * TILE, 4 * TILE), lambda s: (0, s)),
        scratch_shapes=[pltpu.VMEM((JT, KT * TILE, LANES), jnp.bfloat16)],
        compiler_params=pltpu.CompilerParams(vmem_limit_bytes=40 * MIB),
        name="integrals",
    )(k, j, gathered)


def product_kernel(odd_ref, from_ref, lab_ref, tiles_ref, b_ref, other_ref, own_ref, choose, amp, total):
    step = pl.program_id(0)
    groups = QUARTER // tiles_ref.shape[1]

    @pl.when(step == 0)
    def _():
        labels = label_rows(lab_ref[...])
        column = lax.broadcasted_iota(jnp.int32, (1, lab_ref.shape[0]), 1)
        second = ((column & SLOTS) // SLOTS) ^ odd_ref[0]
        k = labels[0:1].astype(jnp.int32) - 1
        i = labels[1:2].astype(jnp.int32)
        cell = k * (2 * VT) + second * VT + i
        row = lax.broadcasted_iota(jnp.int32, choose.shape, 0)
        choose[...] = jnp.where(row == jnp.broadcast_to(cell, choose.shape), 1.0, 0.0).astype(
            jnp.bfloat16
        )

    @pl.when(step < groups)
    def _():
        lane = lax.broadcasted_iota(jnp.int32, (48, LANES), 1)
        lane24 = lax.broadcasted_iota(jnp.int32, (24, LANES), 1)
        count = tiles_ref.shape[1] // 384
        for group in range(count):
            value = jnp.dot(
                choose[...],
                tiles_ref[:, group * 384 : (group + 1) * 384],
                preferred_element_type=jnp.float32,
            )
            for quad in range(KT // 4):
                pieces = []
                for b in range(4):
                    rows = value[(quad * 4 + b) * 24 : (quad * 4 + b + 1) * 24]
                    pieces.append(quad_unpack(rows[:, :128], rows[:, 128:256], rows[:, 256:], lane24))
                base = quad * 384
                for a in (0, 2):
                    w = [
                        jnp.concatenate([turn(pieces[b][a + c], 32 * (a + c - b)) for c in range(2)], axis=0)
                        for b in range(4)
                    ]
                    at = pl.ds(pl.multiple_of(((step * count + group) * 4 + a) * 24, 48), 48)
                    amp[at, base : base + 128] = jnp.where(lane < 96, w[0], w[1]).astype(jnp.bfloat16)
                    amp[at, base + 128 : base + 256] = jnp.where(lane < 64, w[1], w[2]).astype(jnp.bfloat16)
                    amp[at, base + 256 : base + 384] = jnp.where(lane < 32, w[2], w[3]).astype(jnp.bfloat16)

    @pl.when(step >= groups)
    def _():
        size = total.shape[0] * LANES
        for first in range(0, b_ref.shape[1], 256):
            value = jnp.dot(amp[...], b_ref[:, first : first + 256], preferred_element_type=jnp.float32)
            for part in range(2):
                lanes = slice(first + part * LANES, first + (part + 1) * LANES)
                slot = first // LANES + part
                total[slot] = value[:, part * LANES : (part + 1) * LANES]
                for n, ref in ((0, other_ref), (VT, own_ref)):
                    for pair in range(VT // 2):
                        rows = [
                            total[slot, pl.ds(from_ref[n + 2 * pair + q], 24, stride=24), :]
                            for q in range(2)
                        ]
                        ref[pair * 48 : (pair + 1) * 48, lanes] = jnp.concatenate(rows, axis=0).astype(
                            jnp.bfloat16
                        )


def product(odd, rows_from, labelled, label_at, arrived, lanes_at, integrals):
    wide = 768
    groups = QUARTER // wide
    block = 768
    steps = integrals.shape[1] // block
    rows = arrived.shape[0]
    half = VT * TILE // 4
    return pl.pallas_call(
        product_kernel,
        grid=(groups + steps,),
        out_shape=[jax.ShapeDtypeStruct((half, JT * TILE), jnp.bfloat16)] * 2,
        in_specs=[
            pl.BlockSpec(memory_space=pltpu.SMEM),
            pl.BlockSpec(memory_space=pltpu.SMEM),
            pl.BlockSpec((rows, LANES), lambda s: (0, label_at // LANES)),
            pl.BlockSpec((rows, wide), lambda s: (0, lanes_at // wide + jnp.minimum(s, groups - 1))),
            pl.BlockSpec((KT * TILE, block), lambda s: (0, jnp.maximum(s - groups, 0))),
        ],
        out_specs=[pl.BlockSpec((half, block), lambda s: (0, jnp.maximum(s - groups, 0)))] * 2,
        scratch_shapes=[
            pltpu.VMEM((2 * VT * KT, rows), jnp.bfloat16),
            pltpu.VMEM((VT * TILE // 2, KT * TILE), jnp.bfloat16),
            pltpu.VMEM((block // LANES, VT * TILE // 2, LANES), jnp.float32),
        ],
        compiler_params=pltpu.CompilerParams(vmem_limit_bytes=48 * MIB),
        name="product",
    )(odd, rows_from, labelled, arrived, integrals)


def exchange(other, own, ctr_count):
    depth = ctr_count // 2
    swap = [(c, c ^ 1) for c in range(ctr_count)]
    came = lax.ppermute(other, "ctr", swap)
    both = (own.astype(jnp.float32) + came.astype(jnp.float32)).astype(jnp.bfloat16)
    both = both.reshape(depth, -1, own.shape[1])
    total = both[0].astype(jnp.float32)
    parts = []
    for far in (2, 1, 3):
        move = [(c, (c // 2 + far) % depth * 2 + c % 2) for c in range(ctr_count)]
        parts.append(lax.ppermute(both[far], "ctr", move))
    for part in parts:
        total = total + part.astype(jnp.float32)
    return total.astype(jnp.bfloat16)


def lanes_of(columns):
    stacked = jnp.stack(columns, axis=1).astype(jnp.bfloat16)
    return jnp.pad(stacked, ((0, 0), (0, LANES - stacked.shape[1])))


def on_device(amp_tiles, amp_rows, amp_cols, int_tiles, int_rows, int_cols):
    ctr_count = lax.axis_size("ctr")
    devices = lax.axis_size("pair") * ctr_count
    held = amp_tiles.shape[0]
    count = int_rows.shape[1]
    square = int_tiles[0].reshape(count, TILE, TILE).transpose(1, 0, 2).reshape(TILE, count * TILE)
    spare = -(-(count * TILE) // LANES) * LANES - count * TILE
    int_labels = jnp.pad(
        jnp.concatenate([int_rows % KT, int_cols], axis=0).astype(jnp.bfloat16),
        ((0, TILE - 2), (0, spare - count)),
    )
    piece = jnp.concatenate([square, int_labels], axis=1)
    gathered = lax.all_gather(piece, "pair", axis=0, tiled=True)
    names = gathered.reshape(-1, TILE, piece.shape[1])[:, :2, count * TILE : count * TILE + count].astype(jnp.int32)
    target = amp_rows // VT * ctr_count + amp_cols // KT
    order = jnp.arange(held, dtype=jnp.int32)
    earlier = (target[:, None] == target[None, :]) & (order[:, None] < order[None, :])
    land = target * SLOTS + jnp.sum(earlier.astype(jnp.int32), axis=0)
    labels = lanes_of([amp_cols % KT + 1, amp_rows % VT])
    outgoing = pack(land[None, :], labels, amp_tiles, devices)
    arrived = lax.all_to_all(outgoing, ("pair", "ctr"), split_axis=0, concat_axis=0, tiled=True)
    integrals = place_integrals(names[:, 0].reshape(-1), names[:, 1].reshape(-1), gathered)
    ctr = lax.axis_index("ctr").astype(jnp.int32)
    odd, depth = ctr % 2, ctr // 2
    which = jnp.arange(2 * VT, dtype=jnp.int32)
    core = jnp.where(which < VT, 1 - odd, odd)
    owner = (depth + which % VT // 3) % (ctr_count // 2) * 2 + core
    block = 3 * owner + which % 3
    rows_from = block % 2 * VT + block // 2
    halves = []
    for half in range(2):
        other, own = product(odd.reshape(1), rows_from, arrived, HALF, arrived, half * QUARTER, integrals)
        halves.append(exchange(other, own, ctr_count).reshape(3, 24, -1))
    return jnp.stack(halves, axis=1).reshape(144, -1)


def solution(mesh):
    placed = (
        P(("pair", "ctr"), None),
        P(("pair", "ctr")),
        P(("pair", "ctr")),
        P("ctr", "pair", None),
        P("ctr", "pair"),
        P("ctr", "pair"),
    )
    return jax.shard_map(
        on_device, mesh=mesh, in_specs=placed, out_specs=P(("pair", "ctr"), None), check_vma=False
    )
```

```python
import functools

import jax
import jax.numpy as jnp
from jax import lax
from jax.experimental import pallas as pl
from jax.experimental.pallas import tpu as pltpu
from jax.sharding import PartitionSpec as P

TILE = 96
VT = 12
KT = 24
JT = 24
FLAT = TILE * TILE
HALF = FLAT // 2
QUARTER = FLAT // 4
SLOTS = 4
LANES = 128
MIB = 2**20
QUADS = (6, 6)


def quad_unpack(v0, v1, v2, lane):
    return (v0, jnp.where(lane >= 96, v0, v1), jnp.where(lane >= 64, v1, v2), v2)


def turn(x, amount):
    amount = amount % LANES
    return x if amount == 0 else pltpu.roll(x, amount, 1)


def pack_kernel(labelled, land_ref, lab_ref, low_ref, high_ref, out_ref, first, second):
    step = pl.program_id(0)
    rows = first.shape[0]

    @pl.when(step == 0)
    def _():
        row = lax.broadcasted_iota(jnp.int32, first.shape, 0)
        land = jnp.broadcast_to(land_ref[...], first.shape)
        first[...] = jnp.where(row == land, 1.0, 0.0).astype(jnp.bfloat16)
        second[...] = jnp.where((row ^ SLOTS) == land, 1.0, 0.0).astype(jnp.bfloat16)

    def spread(low, high):
        a = jnp.dot(first[...], low, preferred_element_type=jnp.float32)
        b = jnp.dot(second[...], high, preferred_element_type=jnp.float32)
        n = a.shape[1]
        a = a.reshape(rows // 8, 1, 8, n)
        b = b.reshape(rows // 8, 1, 8, n)
        top = lax.broadcasted_iota(jnp.int32, a.shape, 2) < SLOTS
        both = jnp.concatenate([jnp.where(top, a, b), jnp.where(top, b, a)], axis=1)
        return both.reshape(rows * 2, n).astype(jnp.bfloat16)

    if not labelled:
        out_ref[...] = spread(low_ref[...], high_ref[...])
        return

    @pl.when(step < pl.num_programs(0) - 1)
    def _():
        out_ref[...] = spread(low_ref[...], high_ref[...])

    @pl.when(step == pl.num_programs(0) - 1)
    def _():
        out_ref[:, :LANES] = spread(lab_ref[...], lab_ref[...])


def pack(land, labels, tiles, devices, first_quad, quads, labelled):
    held = tiles.shape[0]
    block = 768
    steps = quads * 384 // block
    at = first_quad * 384 // block
    return pl.pallas_call(
        functools.partial(pack_kernel, labelled),
        grid=(steps + int(labelled),),
        out_shape=jax.ShapeDtypeStruct(
            (devices * 2 * SLOTS, quads * 384 + LANES * int(labelled)), jnp.bfloat16
        ),
        in_specs=[
            pl.BlockSpec((1, held), lambda s: (0, 0)),
            pl.BlockSpec((held, LANES), lambda s: (0, 0)),
            pl.BlockSpec((held, block), lambda s: (0, at + jnp.minimum(s, steps - 1))),
            pl.BlockSpec((held, block), lambda s: (0, at + HALF // block + jnp.minimum(s, steps - 1))),
        ],
        out_specs=pl.BlockSpec((devices * 2 * SLOTS, block), lambda s: (0, s)),
        scratch_shapes=[pltpu.VMEM((devices * SLOTS, held), jnp.bfloat16)] * 2,
        compiler_params=pltpu.CompilerParams(vmem_limit_bytes=56 * MIB),
        name="pack",
    )(land, labels, tiles, tiles)


def label_rows(lab):
    unit = (
        lax.broadcasted_iota(jnp.int32, (8, LANES), 0)
        == lax.broadcasted_iota(jnp.int32, (8, LANES), 1)
    )
    return lax.dot_general(
        jnp.where(unit, 1.0, 0.0).astype(jnp.bfloat16),
        lab,
        (((1,), (1,)), ((), ())),
        preferred_element_type=jnp.float32,
    )


def integral_kernel(k_ref, j_ref, tiles_ref, out_ref, spread):
    step = pl.program_id(0)
    held = (tiles_ref.shape[1] - 1) // TILE

    @pl.when(step == 0)
    def _():
        def clear(at, carry):
            spread[at] = jnp.zeros(spread.shape[1:], spread.dtype)
            return carry

        lax.fori_loop(0, JT, clear, 0)
        lane = lax.broadcasted_iota(jnp.int32, (TILE, LANES), 1)

        def source(at, carry):
            rows = pl.ds(pl.multiple_of(at * TILE, TILE), TILE)
            for quad in range(-(-held // 4)):
                v = [
                    tiles_ref[rows, (quad * 3 + n) * LANES : (quad * 3 + n + 1) * LANES].astype(jnp.float32)
                    if (quad * 3 + n) * LANES < tiles_ref.shape[1]
                    else None
                    for n in range(3)
                ]
                v = [v[0] if x is None else x for x in v]
                pieces = quad_unpack(*v, lane)
                for a in range(min(4, held - quad * 4)):
                    k = k_ref[at * held + quad * 4 + a]
                    j = j_ref[at * held + quad * 4 + a]
                    amount = (32 * a + 96 * (j % 4)) % LANES
                    spread[j, pl.ds(pl.multiple_of(k * TILE, TILE), TILE), :] = pltpu.roll(
                        pieces[a], amount, 1
                    ).astype(jnp.bfloat16)
            return carry

        lax.fori_loop(0, tiles_ref.shape[0] // TILE, source, 0)

    size = 256

    def join(at, carry):
        rows = pl.ds(pl.multiple_of(at * size, size), size)
        lane = lax.broadcasted_iota(jnp.int32, (size, LANES), 1)
        w = [spread[step * 4 + b, rows, :].astype(jnp.float32) for b in range(4)]
        out_ref[rows, 0:128] = jnp.where(lane < 96, w[0], w[1]).astype(jnp.bfloat16)
        out_ref[rows, 128:256] = jnp.where(lane < 64, w[1], w[2]).astype(jnp.bfloat16)
        out_ref[rows, 256:384] = jnp.where(lane < 32, w[2], w[3]).astype(jnp.bfloat16)
        return carry

    lax.fori_loop(0, KT * TILE // size, join, 0)


def place_integrals(k, j, gathered):
    return pl.pallas_call(
        integral_kernel,
        grid=(JT // 4,),
        out_shape=jax.ShapeDtypeStruct((KT * TILE, JT * TILE), jnp.bfloat16),
        in_specs=[
            pl.BlockSpec(memory_space=pltpu.SMEM),
            pl.BlockSpec(memory_space=pltpu.SMEM),
            pl.BlockSpec(gathered.shape, lambda s: (0, 0)),
        ],
        out_specs=pl.BlockSpec((KT * TILE, 4 * TILE), lambda s: (0, s)),
        scratch_shapes=[pltpu.VMEM((JT, KT * TILE, LANES), jnp.bfloat16)],
        compiler_params=pltpu.CompilerParams(vmem_limit_bytes=40 * MIB),
        name="integrals",
    )(k, j, gathered)


def choose_kernel(odd_ref, lab_ref, choose_ref):
    labels = label_rows(lab_ref[...])
    column = lax.broadcasted_iota(jnp.int32, (1, lab_ref.shape[0]), 1)
    second = ((column & SLOTS) // SLOTS) ^ odd_ref[0]
    k = labels[0:1].astype(jnp.int32) - 1
    i = labels[1:2].astype(jnp.int32)
    cell = k * (2 * VT) + second * VT + i
    row = lax.broadcasted_iota(jnp.int32, choose_ref.shape, 0)
    choose_ref[...] = jnp.where(row == jnp.broadcast_to(cell, choose_ref.shape), 1.0, 0.0).astype(
        jnp.bfloat16
    )


def choosing(odd, labelled):
    rows = labelled.shape[0]
    return pl.pallas_call(
        choose_kernel,
        grid=(1,),
        out_shape=jax.ShapeDtypeStruct((2 * VT * KT, rows), jnp.bfloat16),
        in_specs=[
            pl.BlockSpec(memory_space=pltpu.SMEM),
            pl.BlockSpec((rows, LANES), lambda s: (0, labelled.shape[1] // LANES - 1)),
        ],
        out_specs=pl.BlockSpec((2 * VT * KT, rows), lambda s: (0, 0)),
        compiler_params=pltpu.CompilerParams(vmem_limit_bytes=58 * MIB),
        name="choose",
    )(odd, labelled)


def place_kernel(choose_ref, tiles_ref, out_ref):
    lane = lax.broadcasted_iota(jnp.int32, (48, LANES), 1)
    lane24 = lax.broadcasted_iota(jnp.int32, (24, LANES), 1)
    for group in range(2):
        value = jnp.dot(
            choose_ref[...],
            tiles_ref[:, group * 384 : (group + 1) * 384],
            preferred_element_type=jnp.float32,
        )
        for quad in range(KT // 4):
            pieces = []
            for b in range(4):
                rows = value[(quad * 4 + b) * 24 : (quad * 4 + b + 1) * 24]
                pieces.append(quad_unpack(rows[:, :128], rows[:, 128:256], rows[:, 256:], lane24))
            base = quad * 384
            for a in (0, 2):
                w = [
                    jnp.concatenate([turn(pieces[b][a + c], 32 * (a + c - b)) for c in range(2)], axis=0)
                    for b in range(4)
                ]
                at = slice((group * 4 + a) * 24, (group * 4 + a) * 24 + 48)
                out_ref[at, base : base + 128] = jnp.where(lane < 96, w[0], w[1]).astype(jnp.bfloat16)
                out_ref[at, base + 128 : base + 256] = jnp.where(lane < 64, w[1], w[2]).astype(jnp.bfloat16)
                out_ref[at, base + 256 : base + 384] = jnp.where(lane < 32, w[2], w[3]).astype(jnp.bfloat16)


def place(choose, arrived, quads):
    return pl.pallas_call(
        place_kernel,
        grid=(quads // 2,),
        out_shape=jax.ShapeDtypeStruct((quads * 96, KT * TILE), jnp.bfloat16),
        in_specs=[
            pl.BlockSpec(choose.shape, lambda s: (0, 0)),
            pl.BlockSpec((arrived.shape[0], 768), lambda s: (0, s)),
        ],
        out_specs=pl.BlockSpec((192, KT * TILE), lambda s: (s, 0)),
        compiler_params=pltpu.CompilerParams(vmem_limit_bytes=58 * MIB),
        name="place",
    )(choose, arrived)


def product_kernel(from_ref, amp_ref, b_ref, *refs):
    outs, total = refs[:-1], refs[-1]
    each = 2 * VT // len(outs)
    depth = amp_ref.shape[0] // (2 * VT)
    joined = 1 if depth % 16 == 0 else 2
    for first in range(0, b_ref.shape[1], 256):
        value = jnp.dot(amp_ref[...], b_ref[:, first : first + 256], preferred_element_type=jnp.float32)
        for part in range(2):
            lanes = slice(first + part * LANES, first + (part + 1) * LANES)
            slot = first // LANES + part
            total[slot] = value[:, part * LANES : (part + 1) * LANES]
            for n, ref in enumerate(outs):
                for at in range(0, each, joined):
                    rows = [
                        total[slot, pl.ds(from_ref[n * each + at + q], depth, stride=2 * VT), :]
                        for q in range(joined)
                    ]
                    ref[at * depth : (at + joined) * depth, lanes] = jnp.concatenate(rows, axis=0).astype(
                        jnp.bfloat16
                    )


def product(rows_from, amp, integrals, outputs):
    block = 768
    size = amp.shape[0] // outputs
    return pl.pallas_call(
        product_kernel,
        grid=(integrals.shape[1] // block,),
        out_shape=[jax.ShapeDtypeStruct((size, JT * TILE), jnp.bfloat16)] * outputs,
        in_specs=[
            pl.BlockSpec(memory_space=pltpu.SMEM),
            pl.BlockSpec(amp.shape, lambda s: (0, 0)),
            pl.BlockSpec((KT * TILE, block), lambda s: (0, s)),
        ],
        out_specs=[pl.BlockSpec((size, block), lambda s: (0, s))] * outputs,
        scratch_shapes=[pltpu.VMEM((block // LANES, amp.shape[0], LANES), jnp.float32)],
        compiler_params=pltpu.CompilerParams(vmem_limit_bytes=58 * MIB),
        name="product",
    )(rows_from, amp, integrals)


def swap_cores(other, own, ctr_count):
    swap = [(c, c ^ 1) for c in range(ctr_count)]
    came = lax.ppermute(other, "ctr", swap)
    return (own.astype(jnp.float32) + came.astype(jnp.float32)).astype(jnp.bfloat16)


def sum_depths(both, ctr_count):
    depth = ctr_count // 2
    both = both.reshape(depth, -1, both.shape[1])
    total = both[0].astype(jnp.float32)
    parts = []
    for far in (2, 1, 3):
        move = [(c, (c // 2 + far) % depth * 2 + c % 2) for c in range(ctr_count)]
        parts.append(lax.ppermute(both[far], "ctr", move))
    for part in parts:
        total = total + part.astype(jnp.float32)
    return total.astype(jnp.bfloat16)


def lanes_of(columns):
    stacked = jnp.stack(columns, axis=1).astype(jnp.bfloat16)
    return jnp.pad(stacked, ((0, 0), (0, LANES - stacked.shape[1])))


def on_device(amp_tiles, amp_rows, amp_cols, int_tiles, int_rows, int_cols):
    ctr_count = lax.axis_size("ctr")
    devices = lax.axis_size("pair") * ctr_count
    held = amp_tiles.shape[0]
    count = int_rows.shape[1]
    square = int_tiles[0].reshape(count, TILE, TILE).transpose(1, 0, 2).reshape(TILE, count * TILE)
    spare = -(-(count * TILE) // LANES) * LANES - count * TILE
    int_labels = jnp.pad(
        jnp.concatenate([int_rows % KT, int_cols], axis=0).astype(jnp.bfloat16),
        ((0, TILE - 2), (0, spare - count)),
    )
    piece = jnp.concatenate([square, int_labels], axis=1)
    gathered = lax.all_gather(piece, "pair", axis=0, tiled=True)
    target = amp_rows // VT * ctr_count + amp_cols // KT
    order = jnp.arange(held, dtype=jnp.int32)
    earlier = (target[:, None] == target[None, :]) & (order[:, None] < order[None, :])
    land = target * SLOTS + jnp.sum(earlier.astype(jnp.int32), axis=0)
    labels = lanes_of([amp_cols % KT + 1, amp_rows % VT])
    everyone = ("pair", "ctr")
    packed = [
        pack(land[None, :], labels, amp_tiles, devices, sum(QUADS[:n]), quads, n == 0)
        for n, quads in enumerate(QUADS)
    ]
    packed = lax.optimization_barrier(packed)
    arrived = [
        lax.all_to_all(outgoing, everyone, split_axis=0, concat_axis=0, tiled=True) for outgoing in packed
    ]
    ctr = lax.axis_index("ctr").astype(jnp.int32)
    odd, depth = ctr % 2, ctr // 2
    which = jnp.arange(2 * VT, dtype=jnp.int32)
    core = jnp.where(which < VT, 1 - odd, odd)
    owner = (depth + which % VT // 3) % (ctr_count // 2) * 2 + core
    block = 3 * owner + which % 3
    spread_rows = block % 2 * VT + block // 2
    block = jnp.arange(2 * VT, dtype=jnp.int32)
    natural_rows = block % 2 * VT + block // 2
    names = gathered.reshape(-1, TILE, piece.shape[1])[:, :2, count * TILE : count * TILE + count]
    names = names.astype(jnp.int32)
    integrals = place_integrals(names[:, 0].reshape(-1), names[:, 1].reshape(-1), gathered)
    arrived[0], integrals = lax.optimization_barrier((arrived[0], integrals))
    choose = choosing(odd.reshape(1), arrived[0])
    parts = []
    for n, quads in enumerate(QUADS):
        amp = place(choose, arrived[n], quads)
        if n < len(QUADS) - 1:
            [value] = product(natural_rows, amp, integrals, 1)
            parts.append(lax.psum_scatter(value, "ctr", scatter_dimension=0, tiled=True))
        else:
            both = swap_cores(*product(spread_rows, amp, integrals, 2), ctr_count)
            parts.append(sum_depths(both, ctr_count))
    parts = [part.reshape(3, quads * 4, -1) for part, quads in zip(parts, QUADS)]
    return jnp.concatenate(parts, axis=1).reshape(144, -1)


def solution(mesh):
    placed = (
        P(("pair", "ctr"), None),
        P(("pair", "ctr")),
        P(("pair", "ctr")),
        P("ctr", "pair", None),
        P("ctr", "pair"),
        P("ctr", "pair"),
    )
    return jax.shard_map(
        on_device, mesh=mesh, in_specs=placed, out_specs=P(("pair", "ctr"), None), check_vma=False
    )
```

```python
import functools

import jax
import jax.numpy as jnp
from jax import lax
from jax.experimental import pallas as pl
from jax.experimental.pallas import tpu as pltpu
from jax.sharding import PartitionSpec as P

TILE = 96
VT = 12
KT = 24
JT = 24
FLAT = TILE * TILE
HALF = FLAT // 2
QUARTER = FLAT // 4
SLOTS = 4
LANES = 128
MIB = 2**20
QUADS = (6, 6)


def quad_unpack(v0, v1, v2, lane):
    return (v0, jnp.where(lane >= 96, v0, v1), jnp.where(lane >= 64, v1, v2), v2)


def turn(x, amount):
    amount = amount % LANES
    return x if amount == 0 else pltpu.roll(x, amount, 1)


def pack_kernel(counts, land_ref, lab_ref, low_ref, high_ref, early_ref, late_ref, first, second):
    step = pl.program_id(0)
    rows = first.shape[0]

    @pl.when(step == 0)
    def _():
        row = lax.broadcasted_iota(jnp.int32, first.shape, 0)
        land = jnp.broadcast_to(land_ref[...], first.shape)
        first[...] = jnp.where(row == land, 1.0, 0.0).astype(jnp.bfloat16)
        second[...] = jnp.where((row ^ SLOTS) == land, 1.0, 0.0).astype(jnp.bfloat16)

    def spread(low, high):
        a = jnp.dot(first[...], low, preferred_element_type=jnp.float32)
        b = jnp.dot(second[...], high, preferred_element_type=jnp.float32)
        n = a.shape[1]
        a = a.reshape(rows // 8, 1, 8, n)
        b = b.reshape(rows // 8, 1, 8, n)
        top = lax.broadcasted_iota(jnp.int32, a.shape, 2) < SLOTS
        both = jnp.concatenate([jnp.where(top, a, b), jnp.where(top, b, a)], axis=1)
        return both.reshape(rows * 2, n).astype(jnp.bfloat16)

    @pl.when(step < counts[0])
    def _():
        early_ref[...] = spread(low_ref[...], high_ref[...])

    @pl.when(step == counts[0])
    def _():
        early_ref[:, :LANES] = spread(lab_ref[...], lab_ref[...])

    @pl.when(step > counts[0])
    def _():
        late_ref[...] = spread(low_ref[...], high_ref[...])


def pack(land, labels, tiles, devices):
    held = tiles.shape[0]
    block = 768
    counts = [quads * 384 // block for quads in QUADS]
    source = lambda s: jnp.minimum(s, counts[0] - 1) + jnp.maximum(s - counts[0], 0)
    rows = devices * 2 * SLOTS
    return pl.pallas_call(
        functools.partial(pack_kernel, counts),
        grid=(sum(counts) + 1,),
        out_shape=[
            jax.ShapeDtypeStruct((rows, QUADS[0] * 384 + LANES), jnp.bfloat16),
            jax.ShapeDtypeStruct((rows, QUADS[1] * 384), jnp.bfloat16),
        ],
        in_specs=[
            pl.BlockSpec((1, held), lambda s: (0, 0)),
            pl.BlockSpec((held, LANES), lambda s: (0, 0)),
            pl.BlockSpec((held, block), lambda s: (0, source(s))),
            pl.BlockSpec((held, block), lambda s: (0, HALF // block + source(s))),
        ],
        out_specs=[
            pl.BlockSpec((rows, block), lambda s: (0, jnp.minimum(s, counts[0]))),
            pl.BlockSpec((rows, block), lambda s: (0, jnp.maximum(s - counts[0] - 1, 0))),
        ],
        scratch_shapes=[pltpu.VMEM((devices * SLOTS, held), jnp.bfloat16)] * 2,
        compiler_params=pltpu.CompilerParams(vmem_limit_bytes=58 * MIB),
        name="pack",
    )(land, labels, tiles, tiles)


def label_rows(lab):
    unit = (
        lax.broadcasted_iota(jnp.int32, (8, LANES), 0)
        == lax.broadcasted_iota(jnp.int32, (8, LANES), 1)
    )
    return lax.dot_general(
        jnp.where(unit, 1.0, 0.0).astype(jnp.bfloat16),
        lab,
        (((1,), (1,)), ((), ())),
        preferred_element_type=jnp.float32,
    )


def integral_kernel(k_ref, j_ref, tiles_ref, out_ref, spread):
    step = pl.program_id(0)
    held = (tiles_ref.shape[1] - 1) // TILE

    @pl.when(step == 0)
    def _():
        def clear(at, carry):
            spread[at] = jnp.zeros(spread.shape[1:], spread.dtype)
            return carry

        lax.fori_loop(0, JT, clear, 0)
        lane = lax.broadcasted_iota(jnp.int32, (TILE, LANES), 1)

        def source(at, carry):
            rows = pl.ds(pl.multiple_of(at * TILE, TILE), TILE)
            for quad in range(-(-held // 4)):
                v = [
                    tiles_ref[rows, (quad * 3 + n) * LANES : (quad * 3 + n + 1) * LANES].astype(jnp.float32)
                    if (quad * 3 + n) * LANES < tiles_ref.shape[1]
                    else None
                    for n in range(3)
                ]
                v = [v[0] if x is None else x for x in v]
                pieces = quad_unpack(*v, lane)
                for a in range(min(4, held - quad * 4)):
                    k = k_ref[at * held + quad * 4 + a]
                    j = j_ref[at * held + quad * 4 + a]
                    amount = (32 * a + 96 * (j % 4)) % LANES
                    spread[j, pl.ds(pl.multiple_of(k * TILE, TILE), TILE), :] = pltpu.roll(
                        pieces[a], amount, 1
                    ).astype(jnp.bfloat16)
            return carry

        lax.fori_loop(0, tiles_ref.shape[0] // TILE, source, 0)

    size = 256

    def join(at, carry):
        rows = pl.ds(pl.multiple_of(at * size, size), size)
        lane = lax.broadcasted_iota(jnp.int32, (size, LANES), 1)
        w = [spread[step * 4 + b, rows, :].astype(jnp.float32) for b in range(4)]
        out_ref[rows, 0:128] = jnp.where(lane < 96, w[0], w[1]).astype(jnp.bfloat16)
        out_ref[rows, 128:256] = jnp.where(lane < 64, w[1], w[2]).astype(jnp.bfloat16)
        out_ref[rows, 256:384] = jnp.where(lane < 32, w[2], w[3]).astype(jnp.bfloat16)
        return carry

    lax.fori_loop(0, KT * TILE // size, join, 0)


def place_integrals(k, j, gathered):
    return pl.pallas_call(
        integral_kernel,
        grid=(JT // 4,),
        out_shape=jax.ShapeDtypeStruct((KT * TILE, JT * TILE), jnp.bfloat16),
        in_specs=[
            pl.BlockSpec(memory_space=pltpu.SMEM),
            pl.BlockSpec(memory_space=pltpu.SMEM),
            pl.BlockSpec(gathered.shape, lambda s: (0, 0)),
        ],
        out_specs=pl.BlockSpec((KT * TILE, 4 * TILE), lambda s: (0, s)),
        scratch_shapes=[pltpu.VMEM((JT, KT * TILE, LANES), jnp.bfloat16)],
        compiler_params=pltpu.CompilerParams(vmem_limit_bytes=38 * MIB),
        name="integrals",
    )(k, j, gathered)


def choose_kernel(odd_ref, lab_ref, choose_ref):
    labels = label_rows(lab_ref[...])
    column = lax.broadcasted_iota(jnp.int32, (1, lab_ref.shape[0]), 1)
    second = ((column & SLOTS) // SLOTS) ^ odd_ref[0]
    k = labels[0:1].astype(jnp.int32) - 1
    i = labels[1:2].astype(jnp.int32)
    cell = k * (2 * VT) + second * VT + i
    row = lax.broadcasted_iota(jnp.int32, choose_ref.shape, 0)
    choose_ref[...] = jnp.where(row == jnp.broadcast_to(cell, choose_ref.shape), 1.0, 0.0).astype(
        jnp.bfloat16
    )


def choosing(odd, labelled):
    rows = labelled.shape[0]
    return pl.pallas_call(
        choose_kernel,
        grid=(1,),
        out_shape=jax.ShapeDtypeStruct((2 * VT * KT, rows), jnp.bfloat16),
        in_specs=[
            pl.BlockSpec(memory_space=pltpu.SMEM),
            pl.BlockSpec((rows, LANES), lambda s: (0, labelled.shape[1] // LANES - 1)),
        ],
        out_specs=pl.BlockSpec((2 * VT * KT, rows), lambda s: (0, 0)),
        compiler_params=pltpu.CompilerParams(vmem_limit_bytes=16 * MIB),
        name="choose",
    )(odd, labelled)


def product_kernel(from_ref, choose_ref, tiles_ref, b_hbm, *refs):
    outs, (amp, total, b_ref, sems) = refs[:-4], refs[-4:]
    step = pl.program_id(0)
    places = amp.shape[0] // 192
    blocks, _, width = b_ref.shape
    copies = [
        pltpu.make_async_copy(b_hbm.at[:, n * width : (n + 1) * width], b_ref.at[n], sems.at[n])
        for n in range(blocks)
    ]

    for n in range(blocks):

        @pl.when(step == min(n, places - 1))
        def _(n=n):
            copies[n].start()

    for n in range(blocks):

        @pl.when(step == places + n)
        def _(n=n):
            copies[n].wait()

    @pl.when(step < places)
    def _():
        lane = lax.broadcasted_iota(jnp.int32, (48, LANES), 1)
        lane24 = lax.broadcasted_iota(jnp.int32, (24, LANES), 1)
        for group in range(2):
            value = jnp.dot(
                choose_ref[...],
                tiles_ref[:, group * 384 : (group + 1) * 384],
                preferred_element_type=jnp.float32,
            )
            for quad in range(KT // 4):
                pieces = []
                for b in range(4):
                    rows = value[(quad * 4 + b) * 24 : (quad * 4 + b + 1) * 24]
                    pieces.append(quad_unpack(rows[:, :128], rows[:, 128:256], rows[:, 256:], lane24))
                base = quad * 384
                for a in (0, 2):
                    w = [
                        jnp.concatenate([turn(pieces[b][a + c], 32 * (a + c - b)) for c in range(2)], axis=0)
                        for b in range(4)
                    ]
                    at = pl.ds(pl.multiple_of(step * 192 + (group * 4 + a) * 24, 48), 48)
                    amp[at, base : base + 128] = jnp.where(lane < 96, w[0], w[1]).astype(jnp.bfloat16)
                    amp[at, base + 128 : base + 256] = jnp.where(lane < 64, w[1], w[2]).astype(jnp.bfloat16)
                    amp[at, base + 256 : base + 384] = jnp.where(lane < 32, w[2], w[3]).astype(jnp.bfloat16)

    each = 2 * VT // len(outs)
    depth = amp.shape[0] // (2 * VT)
    joined = 1 if depth % 16 == 0 else 2

    @pl.when(step >= places)
    def _():
        for first in range(0, width, 256):
            value = jnp.dot(
                amp[...], b_ref[step - places, :, first : first + 256], preferred_element_type=jnp.float32
            )
            for part in range(2):
                lanes = slice(first + part * LANES, first + (part + 1) * LANES)
                slot = first // LANES + part
                total[slot] = value[:, part * LANES : (part + 1) * LANES]
                for n, ref in enumerate(outs):
                    for at in range(0, each, joined):
                        rows = [
                            total[slot, pl.ds(from_ref[n * each + at + q], depth, stride=2 * VT), :]
                            for q in range(joined)
                        ]
                        ref[at * depth : (at + joined) * depth, lanes] = jnp.concatenate(rows, axis=0).astype(
                            jnp.bfloat16
                        )


def product(rows_from, choose, arrived, quads, integrals, outputs):
    block = 768
    places = quads // 2
    height = quads * 96
    size = height // outputs
    late = lambda s: jnp.maximum(s - places, 0)
    return pl.pallas_call(
        product_kernel,
        grid=(places + integrals.shape[1] // block,),
        out_shape=[jax.ShapeDtypeStruct((size, JT * TILE), jnp.bfloat16)] * outputs,
        in_specs=[
            pl.BlockSpec(memory_space=pltpu.SMEM),
            pl.BlockSpec(choose.shape, lambda s: (0, 0)),
            pl.BlockSpec((arrived.shape[0], 768), lambda s: (0, jnp.minimum(s, places - 1))),
            pl.BlockSpec(memory_space=pl.ANY),
        ],
        out_specs=[pl.BlockSpec((size, block), lambda s: (0, late(s)))] * outputs,
        scratch_shapes=[
            pltpu.VMEM((height, KT * TILE), jnp.bfloat16),
            pltpu.VMEM((block // LANES, height, LANES), jnp.float32),
            pltpu.VMEM((integrals.shape[1] // block, KT * TILE, block), jnp.bfloat16),
            pltpu.SemaphoreType.DMA((integrals.shape[1] // block,)),
        ],
        compiler_params=pltpu.CompilerParams(vmem_limit_bytes=58 * MIB),
        name="product",
    )(rows_from, choose, arrived, integrals)


def swap_cores(other, own, ctr_count):
    swap = [(c, c ^ 1) for c in range(ctr_count)]
    came = lax.ppermute(other, "ctr", swap)
    return (own.astype(jnp.float32) + came.astype(jnp.float32)).astype(jnp.bfloat16)


def sum_depths(both, ctr_count):
    depth = ctr_count // 2
    both = both.reshape(depth, -1, both.shape[1])
    total = both[0].astype(jnp.float32)
    parts = []
    for far in (2, 1, 3):
        move = [(c, (c // 2 + far) % depth * 2 + c % 2) for c in range(ctr_count)]
        parts.append(lax.ppermute(both[far], "ctr", move))
    for part in parts:
        total = total + part.astype(jnp.float32)
    return total.astype(jnp.bfloat16)


def lanes_of(columns):
    stacked = jnp.stack(columns, axis=1).astype(jnp.bfloat16)
    return jnp.pad(stacked, ((0, 0), (0, LANES - stacked.shape[1])))


def on_device(amp_tiles, amp_rows, amp_cols, int_tiles, int_rows, int_cols):
    ctr_count = lax.axis_size("ctr")
    devices = lax.axis_size("pair") * ctr_count
    held = amp_tiles.shape[0]
    count = int_rows.shape[1]
    square = int_tiles[0].reshape(count, TILE, TILE).transpose(1, 0, 2).reshape(TILE, count * TILE)
    spare = -(-(count * TILE) // LANES) * LANES - count * TILE
    int_names = jnp.concatenate([int_rows, int_cols], axis=0) % KT
    int_labels = jnp.pad(int_names.astype(jnp.bfloat16), ((0, TILE - 2), (0, spare - count)))
    piece = jnp.concatenate([square, int_labels], axis=1)
    gathered = lax.all_gather(piece, "pair", axis=0, tiled=True)
    target = amp_rows // VT * ctr_count + amp_cols // KT
    order = jnp.arange(held, dtype=jnp.int32)
    earlier = (target[:, None] == target[None, :]) & (order[:, None] < order[None, :])
    land = target * SLOTS + jnp.sum(earlier.astype(jnp.int32), axis=0)
    labels = lanes_of([amp_cols % KT + 1, amp_rows % VT])
    everyone = ("pair", "ctr")
    packed = pack(land[None, :], labels, amp_tiles, devices)
    arrived = [
        lax.all_to_all(outgoing, everyone, split_axis=0, concat_axis=0, tiled=True) for outgoing in packed
    ]
    ctr = lax.axis_index("ctr").astype(jnp.int32)
    odd, depth = ctr % 2, ctr // 2
    which = jnp.arange(2 * VT, dtype=jnp.int32)
    core = jnp.where(which < VT, 1 - odd, odd)
    owner = (depth + which % VT // 3) % (ctr_count // 2) * 2 + core
    block = 3 * owner + which % 3
    spread_rows = block % 2 * VT + block // 2
    block = jnp.arange(2 * VT, dtype=jnp.int32)
    natural_rows = block % 2 * VT + block // 2
    names = gathered.reshape(-1, TILE, piece.shape[1])[:, :2, count * TILE : count * TILE + count]
    names = names.astype(jnp.int32)
    integrals = place_integrals(names[:, 0].reshape(-1), names[:, 1].reshape(-1), gathered)
    arrived[0], integrals = lax.optimization_barrier((arrived[0], integrals))
    choose = choosing(odd.reshape(1), arrived[0])
    parts = []
    for n, quads in enumerate(QUADS):
        if n < len(QUADS) - 1:
            [value] = product(natural_rows, choose, arrived[n], quads, integrals, 1)
            parts.append(lax.psum_scatter(value, "ctr", scatter_dimension=0, tiled=True))
        else:
            both = swap_cores(*product(spread_rows, choose, arrived[n], quads, integrals, 2), ctr_count)
            parts.append(sum_depths(both, ctr_count))
    parts = [part.reshape(3, quads * 4, -1) for part, quads in zip(parts, QUADS)]
    return jnp.concatenate(parts, axis=1).reshape(144, -1)


def solution(mesh):
    placed = (
        P(("pair", "ctr"), None),
        P(("pair", "ctr")),
        P(("pair", "ctr")),
        P("ctr", "pair", None),
        P("ctr", "pair"),
        P("ctr", "pair"),
    )
    return jax.shard_map(
        on_device, mesh=mesh, in_specs=placed, out_specs=P(("pair", "ctr"), None), check_vma=False
    )
```

```python
import functools

import jax
import jax.numpy as jnp
from jax import lax
from jax.experimental import pallas as pl
from jax.experimental.pallas import tpu as pltpu
from jax.sharding import PartitionSpec as P

TILE = 96
VT = 12
KT = 24
JT = 24
FLAT = TILE * TILE
HALF = FLAT // 2
QUARTER = FLAT // 4
SLOTS = 4
LANES = 128
MIB = 2**20
QUADS = (8, 4)


def quad_unpack(v0, v1, v2, lane):
    return (v0, jnp.where(lane >= 96, v0, v1), jnp.where(lane >= 64, v1, v2), v2)


def turn(x, amount):
    amount = amount % LANES
    return x if amount == 0 else pltpu.roll(x, amount, 1)


def pack_kernel(counts, land_ref, lab_ref, low_ref, high_ref, early_ref, late_ref, first, second):
    step = pl.program_id(0)
    rows = first.shape[0]

    @pl.when(step == 0)
    def _():
        row = lax.broadcasted_iota(jnp.int32, first.shape, 0)
        land = jnp.broadcast_to(land_ref[...], first.shape)
        first[...] = jnp.where(row == land, 1.0, 0.0).astype(jnp.bfloat16)
        second[...] = jnp.where((row ^ SLOTS) == land, 1.0, 0.0).astype(jnp.bfloat16)

    def spread(low, high):
        a = jnp.dot(first[...], low, preferred_element_type=jnp.float32)
        b = jnp.dot(second[...], high, preferred_element_type=jnp.float32)
        n = a.shape[1]
        a = a.reshape(rows // 8, 1, 8, n)
        b = b.reshape(rows // 8, 1, 8, n)
        top = lax.broadcasted_iota(jnp.int32, a.shape, 2) < SLOTS
        both = jnp.concatenate([jnp.where(top, a, b), jnp.where(top, b, a)], axis=1)
        return both.reshape(rows * 2, n).astype(jnp.bfloat16)

    @pl.when(step < counts[0])
    def _():
        early_ref[...] = spread(low_ref[...], high_ref[...])

    @pl.when(step == counts[0])
    def _():
        early_ref[:, :LANES] = spread(lab_ref[...], lab_ref[...])

    @pl.when(step > counts[0])
    def _():
        late_ref[...] = spread(low_ref[...], high_ref[...])


def pack(land, labels, tiles, devices):
    held = tiles.shape[0]
    block = 768
    counts = [quads * 384 // block for quads in QUADS]
    source = lambda s: jnp.minimum(s, counts[0] - 1) + jnp.maximum(s - counts[0], 0)
    rows = devices * 2 * SLOTS
    return pl.pallas_call(
        functools.partial(pack_kernel, counts),
        grid=(sum(counts) + 1,),
        out_shape=[
            jax.ShapeDtypeStruct((rows, QUADS[0] * 384 + LANES), jnp.bfloat16),
            jax.ShapeDtypeStruct((rows, QUADS[1] * 384), jnp.bfloat16),
        ],
        in_specs=[
            pl.BlockSpec((1, held), lambda s: (0, 0)),
            pl.BlockSpec((held, LANES), lambda s: (0, 0)),
            pl.BlockSpec((held, block), lambda s: (0, source(s))),
            pl.BlockSpec((held, block), lambda s: (0, HALF // block + source(s))),
        ],
        out_specs=[
            pl.BlockSpec((rows, block), lambda s: (0, jnp.minimum(s, counts[0]))),
            pl.BlockSpec((rows, block), lambda s: (0, jnp.maximum(s - counts[0] - 1, 0))),
        ],
        scratch_shapes=[pltpu.VMEM((devices * SLOTS, held), jnp.bfloat16)] * 2,
        compiler_params=pltpu.CompilerParams(vmem_limit_bytes=58 * MIB),
        name="pack",
    )(land, labels, tiles, tiles)


def label_rows(lab):
    unit = (
        lax.broadcasted_iota(jnp.int32, (8, LANES), 0)
        == lax.broadcasted_iota(jnp.int32, (8, LANES), 1)
    )
    return lax.dot_general(
        jnp.where(unit, 1.0, 0.0).astype(jnp.bfloat16),
        lab,
        (((1,), (1,)), ((), ())),
        preferred_element_type=jnp.float32,
    )


def integral_kernel(names_ref, tiles_hbm, out_ref, tiles_ref, spread, sem):
    step = pl.program_id(0)
    sources, _, held = names_ref.shape

    @pl.when(step == 0)
    def _():
        copy = pltpu.make_async_copy(tiles_hbm, tiles_ref, sem)
        copy.start()

        def clear(at, carry):
            spread[at] = jnp.zeros(spread.shape[1:], spread.dtype)
            return carry

        lax.fori_loop(0, JT, clear, 0)
        copy.wait()
        lane = lax.broadcasted_iota(jnp.int32, (TILE, LANES), 1)

        def source(at, carry):
            rows = pl.ds(pl.multiple_of(at * TILE, TILE), TILE)
            for quad in range(-(-held // 4)):
                v = [
                    tiles_ref[rows, (quad * 3 + n) * LANES : (quad * 3 + n + 1) * LANES].astype(jnp.float32)
                    if (quad * 3 + n) * LANES < tiles_ref.shape[1]
                    else None
                    for n in range(3)
                ]
                v = [v[0] if x is None else x for x in v]
                pieces = quad_unpack(*v, lane)
                for a in range(min(4, held - quad * 4)):
                    k = names_ref[at, 0, quad * 4 + a]
                    j = names_ref[at, 1, quad * 4 + a]
                    amount = (32 * a + 96 * (j % 4)) % LANES
                    spread[j, pl.ds(pl.multiple_of(k * TILE, TILE), TILE), :] = pltpu.roll(
                        pieces[a], amount, 1
                    ).astype(jnp.bfloat16)
            return carry

        lax.fori_loop(0, sources, source, 0)

    size = 256

    def join(at, carry):
        rows = pl.ds(pl.multiple_of(at * size, size), size)
        lane = lax.broadcasted_iota(jnp.int32, (size, LANES), 1)
        w = [spread[step * 4 + b, rows, :].astype(jnp.float32) for b in range(4)]
        out_ref[rows, 0:128] = jnp.where(lane < 96, w[0], w[1]).astype(jnp.bfloat16)
        out_ref[rows, 128:256] = jnp.where(lane < 64, w[1], w[2]).astype(jnp.bfloat16)
        out_ref[rows, 256:384] = jnp.where(lane < 32, w[2], w[3]).astype(jnp.bfloat16)
        return carry

    lax.fori_loop(0, KT * TILE // size, join, 0)


def place_integrals(names, gathered):
    return pl.pallas_call(
        integral_kernel,
        grid=(JT // 4,),
        out_shape=jax.ShapeDtypeStruct((KT * TILE, JT * TILE), jnp.bfloat16),
        in_specs=[
            pl.BlockSpec(memory_space=pltpu.SMEM),
            pl.BlockSpec(memory_space=pl.ANY),
        ],
        out_specs=pl.BlockSpec((KT * TILE, 4 * TILE), lambda s: (0, s)),
        scratch_shapes=[
            pltpu.VMEM(gathered.shape, jnp.bfloat16),
            pltpu.VMEM((JT, KT * TILE, LANES), jnp.bfloat16),
            pltpu.SemaphoreType.DMA,
        ],
        compiler_params=pltpu.CompilerParams(vmem_limit_bytes=60 * MIB),
        name="integrals",
    )(names, gathered)


def product_kernel(depths, ctr_ref, lab_ref, tiles_ref, b_hbm, *refs):
    outs, (choose, amp, total, b_ref, sems) = refs[:-5], refs[-5:]
    step = pl.program_id(0)
    places = amp.shape[0] // 192
    blocks, _, width = b_ref.shape
    odd, layer = ctr_ref[0] & 1, ctr_ref[0] >> 1
    copies = [
        pltpu.make_async_copy(b_hbm.at[:, n * width : (n + 1) * width], b_ref.at[n], sems.at[n])
        for n in range(blocks)
    ]

    def row_of(n, at):
        block = at
        if len(outs) == 2:
            core = odd if n == 1 else 1 - odd
            block = ((layer + at // 3) % depths * 2 + core) * 3 + at % 3
        return (block & 1) * VT + (block >> 1)

    @pl.when(step == 0)
    def _():
        labels = label_rows(lab_ref[...])
        column = lax.broadcasted_iota(jnp.int32, (1, lab_ref.shape[0]), 1)
        second = ((column & SLOTS) // SLOTS) ^ odd
        k = labels[0:1].astype(jnp.int32) - 1
        i = labels[1:2].astype(jnp.int32)
        cell = k * (2 * VT) + second * VT + i
        row = lax.broadcasted_iota(jnp.int32, choose.shape, 0)
        choose[...] = jnp.where(row == jnp.broadcast_to(cell, choose.shape), 1.0, 0.0).astype(
            jnp.bfloat16
        )

    for n in range(blocks):

        @pl.when(step == min(n, places - 1))
        def _(n=n):
            copies[n].start()

    for n in range(blocks):

        @pl.when(step == places + n)
        def _(n=n):
            copies[n].wait()

    @pl.when(step < places)
    def _():
        lane = lax.broadcasted_iota(jnp.int32, (48, LANES), 1)
        lane24 = lax.broadcasted_iota(jnp.int32, (24, LANES), 1)
        for group in range(2):
            value = jnp.dot(
                choose[...],
                tiles_ref[:, group * 384 : (group + 1) * 384],
                preferred_element_type=jnp.float32,
            )
            for quad in range(KT // 4):
                pieces = []
                for b in range(4):
                    rows = value[(quad * 4 + b) * 24 : (quad * 4 + b + 1) * 24]
                    pieces.append(quad_unpack(rows[:, :128], rows[:, 128:256], rows[:, 256:], lane24))
                base = quad * 384
                for a in (0, 2):
                    w = [
                        jnp.concatenate([turn(pieces[b][a + c], 32 * (a + c - b)) for c in range(2)], axis=0)
                        for b in range(4)
                    ]
                    at = pl.ds(pl.multiple_of(step * 192 + (group * 4 + a) * 24, 48), 48)
                    amp[at, base : base + 128] = jnp.where(lane < 96, w[0], w[1]).astype(jnp.bfloat16)
                    amp[at, base + 128 : base + 256] = jnp.where(lane < 64, w[1], w[2]).astype(jnp.bfloat16)
                    amp[at, base + 256 : base + 384] = jnp.where(lane < 32, w[2], w[3]).astype(jnp.bfloat16)

    each = 2 * VT // len(outs)
    depth = amp.shape[0] // (2 * VT)
    joined = 1 if depth % 16 == 0 else 2

    @pl.when(step >= places)
    def _():
        for first in range(0, width, 256):
            value = jnp.dot(
                amp[...], b_ref[step - places, :, first : first + 256], preferred_element_type=jnp.float32
            )
            for part in range(2):
                lanes = slice(first + part * LANES, first + (part + 1) * LANES)
                slot = first // LANES + part
                total[slot] = value[:, part * LANES : (part + 1) * LANES]
                for n, ref in enumerate(outs):
                    for at in range(0, each, joined):
                        rows = [
                            total[slot, pl.ds(row_of(n, at + q), depth, stride=2 * VT), :]
                            for q in range(joined)
                        ]
                        ref[at * depth : (at + joined) * depth, lanes] = jnp.concatenate(rows, axis=0).astype(
                            jnp.bfloat16
                        )


def product(ctr, labelled, arrived, quads, integrals, outputs, depths):
    block = 768
    blocks = integrals.shape[1] // block
    places = quads // 2
    height = quads * 96
    size = height // outputs
    rows = arrived.shape[0]
    flops = 10**6 if outputs == 1 else 10**11
    late = lambda s: jnp.maximum(s - places, 0)
    return pl.pallas_call(
        functools.partial(product_kernel, depths),
        grid=(places + blocks,),
        out_shape=[jax.ShapeDtypeStruct((size, JT * TILE), jnp.bfloat16)] * outputs,
        in_specs=[
            pl.BlockSpec(memory_space=pltpu.SMEM),
            pl.BlockSpec((rows, LANES), lambda s: (0, labelled.shape[1] // LANES - 1)),
            pl.BlockSpec((rows, 768), lambda s: (0, jnp.minimum(s, places - 1))),
            pl.BlockSpec(memory_space=pl.ANY),
        ],
        out_specs=[pl.BlockSpec((size, block), lambda s: (0, late(s)))] * outputs,
        scratch_shapes=[
            pltpu.VMEM((2 * VT * KT, rows), jnp.bfloat16),
            pltpu.VMEM((height, KT * TILE), jnp.bfloat16),
            pltpu.VMEM((block // LANES, height, LANES), jnp.float32),
            pltpu.VMEM((blocks, KT * TILE, block), jnp.bfloat16),
            pltpu.SemaphoreType.DMA((blocks,)),
        ],
        compiler_params=pltpu.CompilerParams(vmem_limit_bytes=61 * MIB),
        cost_estimate=pl.CostEstimate(flops=flops, bytes_accessed=flops // 300, transcendentals=0),
        name="product",
    )(ctr, labelled, arrived, integrals)


def swap_cores(other, own, ctr_count):
    swap = [(c, c ^ 1) for c in range(ctr_count)]
    came = lax.ppermute(other, "ctr", swap)
    return (own.astype(jnp.float32) + came.astype(jnp.float32)).astype(jnp.bfloat16)


def sum_depths(both, ctr_count):
    depth = ctr_count // 2
    both = both.reshape(depth, -1, both.shape[1])
    total = both[0].astype(jnp.float32)
    parts = []
    for far in (2, 1, 3):
        move = [(c, (c // 2 + far) % depth * 2 + c % 2) for c in range(ctr_count)]
        parts.append(lax.ppermute(both[far], "ctr", move))
    for part in parts:
        total = total + part.astype(jnp.float32)
    return total.astype(jnp.bfloat16)


def lanes_of(columns):
    stacked = jnp.stack(columns, axis=1).astype(jnp.bfloat16)
    return jnp.pad(stacked, ((0, 0), (0, LANES - stacked.shape[1])))


def on_device(amp_tiles, amp_rows, amp_cols, int_tiles, int_rows, int_cols):
    ctr_count = lax.axis_size("ctr")
    devices = lax.axis_size("pair") * ctr_count
    held = amp_tiles.shape[0]
    count = int_rows.shape[1]
    square = int_tiles[0].reshape(count, TILE, TILE).transpose(1, 0, 2).reshape(TILE, count * TILE)
    spare = -(-(count * TILE) // LANES) * LANES - count * TILE
    int_names = jnp.concatenate([int_rows, int_cols], axis=0) % KT
    int_labels = jnp.pad(int_names.astype(jnp.bfloat16), ((0, TILE - 2), (0, spare - count)))
    piece = jnp.concatenate([square, int_labels], axis=1)
    gathered = lax.all_gather(piece, "pair", axis=0, tiled=True)
    target = amp_rows // VT * ctr_count + amp_cols // KT
    order = jnp.arange(held, dtype=jnp.int32)
    earlier = (target[:, None] == target[None, :]) & (order[:, None] < order[None, :])
    land = target * SLOTS + jnp.sum(earlier.astype(jnp.int32), axis=0)
    labels = lanes_of([amp_cols % KT + 1, amp_rows % VT])
    everyone = ("pair", "ctr")
    packed = pack(land[None, :], labels, amp_tiles, devices)
    arrived = [
        lax.all_to_all(outgoing, everyone, split_axis=0, concat_axis=0, tiled=True) for outgoing in packed
    ]
    ctr = lax.axis_index("ctr").astype(jnp.int32).reshape(1)
    names = gathered.reshape(-1, TILE, piece.shape[1])[:, :2, count * TILE : count * TILE + count]
    integrals = place_integrals(names.astype(jnp.int32), gathered)
    arrived[0], integrals = lax.optimization_barrier((arrived[0], integrals))
    parts = []
    for n, quads in enumerate(QUADS):
        if n < len(QUADS) - 1:
            [value] = product(ctr, arrived[0], arrived[n], quads, integrals, 1, ctr_count // 2)
            parts.append(lax.psum_scatter(value, "ctr", scatter_dimension=0, tiled=True))
        else:
            both = swap_cores(
                *product(ctr, arrived[0], arrived[n], quads, integrals, 2, ctr_count // 2), ctr_count
            )
            parts.append(sum_depths(both, ctr_count))
    parts = [part.reshape(3, quads * 4, -1) for part, quads in zip(parts, QUADS)]
    return jnp.concatenate(parts, axis=1).reshape(144, -1)


def solution(mesh):
    placed = (
        P(("pair", "ctr"), None),
        P(("pair", "ctr")),
        P(("pair", "ctr")),
        P("ctr", "pair", None),
        P("ctr", "pair"),
        P("ctr", "pair"),
    )
    return jax.shard_map(
        on_device, mesh=mesh, in_specs=placed, out_specs=P(("pair", "ctr"), None), check_vma=False
    )
```

```python
import functools

import jax
import jax.numpy as jnp
from jax import lax
from jax.experimental import pallas as pl
from jax.experimental.pallas import tpu as pltpu
from jax.sharding import PartitionSpec as P

TILE = 96
VT = 12
KT = 24
JT = 24
FLAT = TILE * TILE
HALF = FLAT // 2
QUARTER = FLAT // 4
SLOTS = 4
LANES = 128
MIB = 2**20
QUADS = (8, 4)


def quad_unpack(v0, v1, v2, lane):
    return (v0, jnp.where(lane >= 96, v0, v1), jnp.where(lane >= 64, v1, v2), v2)


def turn(x, amount):
    amount = amount % LANES
    return x if amount == 0 else pltpu.roll(x, amount, 1)


def pack_kernel(counts, target_ref, k_ref, i_ref, low_ref, high_ref, early_ref, late_ref, first, second):
    step = pl.program_id(0)
    rows = first.shape[0]

    @pl.when(step == 0)
    def _():
        row = lax.broadcasted_iota(jnp.int32, first.shape, 0)
        held = target_ref.shape[1]
        across = jnp.broadcast_to(target_ref[...], (held, held))
        down = jnp.transpose(across)
        before = lax.broadcasted_iota(jnp.int32, across.shape, 0) < lax.broadcasted_iota(
            jnp.int32, across.shape, 1
        )
        rank = jnp.sum(jnp.where((across == down) & before, 1, 0), axis=0, keepdims=True)
        land = jnp.broadcast_to(target_ref[...] * SLOTS + rank, first.shape)
        first[...] = jnp.where(row == land, 1.0, 0.0).astype(jnp.bfloat16)
        second[...] = jnp.where((row ^ SLOTS) == land, 1.0, 0.0).astype(jnp.bfloat16)

    def spread(low, high, side=0):
        dims = (((1,), (side,)), ((), ()))
        a = lax.dot_general(first[...], low, dims, preferred_element_type=jnp.float32)
        b = lax.dot_general(second[...], high, dims, preferred_element_type=jnp.float32)
        n = a.shape[1]
        a = a.reshape(rows // 8, 1, 8, n)
        b = b.reshape(rows // 8, 1, 8, n)
        top = lax.broadcasted_iota(jnp.int32, a.shape, 2) < SLOTS
        both = jnp.concatenate([jnp.where(top, a, b), jnp.where(top, b, a)], axis=1)
        return both.reshape(rows * 2, n).astype(jnp.bfloat16)

    @pl.when(step < counts[0])
    def _():
        early_ref[...] = spread(low_ref[...], high_ref[...])

    @pl.when(step == counts[0])
    def _():
        shape = (LANES, k_ref.shape[1])
        kind = lax.broadcasted_iota(jnp.int32, shape, 0)
        k = jnp.broadcast_to(k_ref[...] + 1, shape)
        i = jnp.broadcast_to(i_ref[...], shape)
        labels = jnp.where(kind == 0, k, jnp.where(kind == 1, i, 0))
        labels = labels.astype(jnp.float32).astype(jnp.bfloat16)
        early_ref[:, :LANES] = spread(labels, labels, 1)

    @pl.when(step > counts[0])
    def _():
        late_ref[...] = spread(low_ref[...], high_ref[...])


def pack(target, k, i, tiles, devices):
    held = tiles.shape[0]
    block = 768
    counts = [quads * 384 // block for quads in QUADS]
    source = lambda s: jnp.minimum(s, counts[0] - 1) + jnp.maximum(s - counts[0], 0)
    rows = devices * 2 * SLOTS
    return pl.pallas_call(
        functools.partial(pack_kernel, counts),
        grid=(sum(counts) + 1,),
        out_shape=[
            jax.ShapeDtypeStruct((rows, QUADS[0] * 384 + LANES), jnp.bfloat16),
            jax.ShapeDtypeStruct((rows, QUADS[1] * 384), jnp.bfloat16),
        ],
        in_specs=[
            pl.BlockSpec((1, held), lambda s: (0, 0)),
            pl.BlockSpec((1, held), lambda s: (0, 0)),
            pl.BlockSpec((1, held), lambda s: (0, 0)),
            pl.BlockSpec((held, block), lambda s: (0, source(s))),
            pl.BlockSpec((held, block), lambda s: (0, HALF // block + source(s))),
        ],
        out_specs=[
            pl.BlockSpec((rows, block), lambda s: (0, jnp.minimum(s, counts[0]))),
            pl.BlockSpec((rows, block), lambda s: (0, jnp.maximum(s - counts[0] - 1, 0))),
        ],
        scratch_shapes=[pltpu.VMEM((devices * SLOTS, held), jnp.bfloat16)] * 2,
        compiler_params=pltpu.CompilerParams(vmem_limit_bytes=58 * MIB),
        name="pack",
    )(target[None, :], k[None, :], i[None, :], tiles, tiles)


def label_rows(lab):
    unit = (
        lax.broadcasted_iota(jnp.int32, (8, LANES), 0)
        == lax.broadcasted_iota(jnp.int32, (8, LANES), 1)
    )
    return lax.dot_general(
        jnp.where(unit, 1.0, 0.0).astype(jnp.bfloat16),
        lab,
        (((1,), (1,)), ((), ())),
        preferred_element_type=jnp.float32,
    )


def integral_kernel(names_ref, tiles_hbm, out_ref, tiles_ref, spread, sem):
    step = pl.program_id(0)
    sources, _, held = names_ref.shape

    @pl.when(step == 0)
    def _():
        copy = pltpu.make_async_copy(tiles_hbm, tiles_ref, sem)
        copy.start()

        def clear(at, carry):
            spread[at] = jnp.zeros(spread.shape[1:], spread.dtype)
            return carry

        lax.fori_loop(0, JT, clear, 0)
        copy.wait()
        lane = lax.broadcasted_iota(jnp.int32, (TILE, LANES), 1)

        def source(at, carry):
            rows = pl.ds(pl.multiple_of(at * TILE, TILE), TILE)
            for quad in range(-(-held // 4)):
                v = [
                    tiles_ref[rows, (quad * 3 + n) * LANES : (quad * 3 + n + 1) * LANES].astype(jnp.float32)
                    if (quad * 3 + n) * LANES < tiles_ref.shape[1]
                    else None
                    for n in range(3)
                ]
                v = [v[0] if x is None else x for x in v]
                pieces = quad_unpack(*v, lane)
                for a in range(min(4, held - quad * 4)):
                    k = names_ref[at, 0, quad * 4 + a]
                    j = names_ref[at, 1, quad * 4 + a]
                    amount = (32 * a + 96 * (j % 4)) % LANES
                    spread[j, pl.ds(pl.multiple_of(k * TILE, TILE), TILE), :] = pltpu.roll(
                        pieces[a], amount, 1
                    ).astype(jnp.bfloat16)
            return carry

        lax.fori_loop(0, sources, source, 0)

    size = 256

    def join(at, carry):
        rows = pl.ds(pl.multiple_of(at * size, size), size)
        lane = lax.broadcasted_iota(jnp.int32, (size, LANES), 1)
        w = [spread[step * 4 + b, rows, :].astype(jnp.float32) for b in range(4)]
        out_ref[rows, 0:128] = jnp.where(lane < 96, w[0], w[1]).astype(jnp.bfloat16)
        out_ref[rows, 128:256] = jnp.where(lane < 64, w[1], w[2]).astype(jnp.bfloat16)
        out_ref[rows, 256:384] = jnp.where(lane < 32, w[2], w[3]).astype(jnp.bfloat16)
        return carry

    lax.fori_loop(0, KT * TILE // size, join, 0)


def place_integrals(names, gathered):
    return pl.pallas_call(
        integral_kernel,
        grid=(JT // 4,),
        out_shape=jax.ShapeDtypeStruct((KT * TILE, JT * TILE), jnp.bfloat16),
        in_specs=[
            pl.BlockSpec(memory_space=pltpu.SMEM),
            pl.BlockSpec(memory_space=pl.ANY),
        ],
        out_specs=pl.BlockSpec((KT * TILE, 4 * TILE), lambda s: (0, s)),
        scratch_shapes=[
            pltpu.VMEM(gathered.shape, jnp.bfloat16),
            pltpu.VMEM((JT, KT * TILE, LANES), jnp.bfloat16),
            pltpu.SemaphoreType.DMA,
        ],
        compiler_params=pltpu.CompilerParams(vmem_limit_bytes=60 * MIB),
        name="integrals",
    )(names, gathered)


def product_kernel(depths, ctr_ref, lab_ref, tiles_ref, b_hbm, *refs):
    outs, (choose, amp, total, b_ref, sems) = refs[:-5], refs[-5:]
    step = pl.program_id(0)
    places = amp.shape[0] // 192
    blocks, _, width = b_ref.shape
    odd, layer = ctr_ref[0] & 1, ctr_ref[0] >> 1
    copies = [
        pltpu.make_async_copy(b_hbm.at[:, n * width : (n + 1) * width], b_ref.at[n], sems.at[n])
        for n in range(blocks)
    ]

    def row_of(n, at):
        block = at
        if len(outs) == 2:
            core = odd if n == 1 else 1 - odd
            block = ((layer + at // 3) % depths * 2 + core) * 3 + at % 3
        return (block & 1) * VT + (block >> 1)

    @pl.when(step == 0)
    def _():
        labels = label_rows(lab_ref[...])
        column = lax.broadcasted_iota(jnp.int32, (1, lab_ref.shape[0]), 1)
        second = ((column & SLOTS) // SLOTS) ^ odd
        k = labels[0:1].astype(jnp.int32) - 1
        i = labels[1:2].astype(jnp.int32)
        cell = k * (2 * VT) + second * VT + i
        row = lax.broadcasted_iota(jnp.int32, choose.shape, 0)
        choose[...] = jnp.where(row == jnp.broadcast_to(cell, choose.shape), 1.0, 0.0).astype(
            jnp.bfloat16
        )

    for n in range(blocks):

        @pl.when(step == min(n, places - 1))
        def _(n=n):
            copies[n].start()

    for n in range(blocks):

        @pl.when(step == places + n)
        def _(n=n):
            copies[n].wait()

    @pl.when(step < places)
    def _():
        lane = lax.broadcasted_iota(jnp.int32, (48, LANES), 1)
        lane24 = lax.broadcasted_iota(jnp.int32, (24, LANES), 1)
        for group in range(2):
            value = jnp.dot(
                choose[...],
                tiles_ref[:, group * 384 : (group + 1) * 384],
                preferred_element_type=jnp.float32,
            )
            for quad in range(KT // 4):
                pieces = []
                for b in range(4):
                    rows = value[(quad * 4 + b) * 24 : (quad * 4 + b + 1) * 24]
                    pieces.append(quad_unpack(rows[:, :128], rows[:, 128:256], rows[:, 256:], lane24))
                base = quad * 384
                for a in (0, 2):
                    w = [
                        jnp.concatenate([turn(pieces[b][a + c], 32 * (a + c - b)) for c in range(2)], axis=0)
                        for b in range(4)
                    ]
                    at = pl.ds(pl.multiple_of(step * 192 + (group * 4 + a) * 24, 48), 48)
                    amp[at, base : base + 128] = jnp.where(lane < 96, w[0], w[1]).astype(jnp.bfloat16)
                    amp[at, base + 128 : base + 256] = jnp.where(lane < 64, w[1], w[2]).astype(jnp.bfloat16)
                    amp[at, base + 256 : base + 384] = jnp.where(lane < 32, w[2], w[3]).astype(jnp.bfloat16)

    each = 2 * VT // len(outs)
    depth = amp.shape[0] // (2 * VT)
    joined = 1 if depth % 16 == 0 else 2

    @pl.when(step >= places)
    def _():
        for first in range(0, width, 256):
            value = jnp.dot(
                amp[...], b_ref[step - places, :, first : first + 256], preferred_element_type=jnp.float32
            )
            for part in range(2):
                lanes = slice(first + part * LANES, first + (part + 1) * LANES)
                slot = first // LANES + part
                total[slot] = value[:, part * LANES : (part + 1) * LANES]
                for n, ref in enumerate(outs):
                    for at in range(0, each, joined):
                        rows = [
                            total[slot, pl.ds(row_of(n, at + q), depth, stride=2 * VT), :]
                            for q in range(joined)
                        ]
                        ref[at * depth : (at + joined) * depth, lanes] = jnp.concatenate(rows, axis=0).astype(
                            jnp.bfloat16
                        )


def product(ctr, labelled, arrived, quads, integrals, outputs, depths):
    block = 768
    blocks = integrals.shape[1] // block
    places = quads // 2
    height = quads * 96
    size = height // outputs
    rows = arrived.shape[0]
    flops = 10**6 if outputs == 1 else 10**11
    late = lambda s: jnp.maximum(s - places, 0)
    return pl.pallas_call(
        functools.partial(product_kernel, depths),
        grid=(places + blocks,),
        out_shape=[jax.ShapeDtypeStruct((size, JT * TILE), jnp.bfloat16)] * outputs,
        in_specs=[
            pl.BlockSpec(memory_space=pltpu.SMEM),
            pl.BlockSpec((rows, LANES), lambda s: (0, labelled.shape[1] // LANES - 1)),
            pl.BlockSpec((rows, 768), lambda s: (0, jnp.minimum(s, places - 1))),
            pl.BlockSpec(memory_space=pl.ANY),
        ],
        out_specs=[pl.BlockSpec((size, block), lambda s: (0, late(s)))] * outputs,
        scratch_shapes=[
            pltpu.VMEM((2 * VT * KT, rows), jnp.bfloat16),
            pltpu.VMEM((height, KT * TILE), jnp.bfloat16),
            pltpu.VMEM((block // LANES, height, LANES), jnp.float32),
            pltpu.VMEM((blocks, KT * TILE, block), jnp.bfloat16),
            pltpu.SemaphoreType.DMA((blocks,)),
        ],
        compiler_params=pltpu.CompilerParams(vmem_limit_bytes=61 * MIB),
        cost_estimate=pl.CostEstimate(flops=flops, bytes_accessed=flops // 300, transcendentals=0),
        name="product",
    )(ctr, labelled, arrived, integrals)


def swap_cores(other, own, ctr_count):
    swap = [(c, c ^ 1) for c in range(ctr_count)]
    came = lax.ppermute(other, "ctr", swap)
    return (own.astype(jnp.float32) + came.astype(jnp.float32)).astype(jnp.bfloat16)


def sum_depths(both, ctr_count):
    depth = ctr_count // 2
    both = both.reshape(depth, -1, both.shape[1])
    total = both[0].astype(jnp.float32)
    parts = []
    for far in (2, 1, 3):
        move = [(c, (c // 2 + far) % depth * 2 + c % 2) for c in range(ctr_count)]
        parts.append(lax.ppermute(both[far], "ctr", move))
    for part in parts:
        total = total + part.astype(jnp.float32)
    return total.astype(jnp.bfloat16)


def on_device(amp_tiles, amp_rows, amp_cols, int_tiles, int_rows, int_cols):
    ctr_count = lax.axis_size("ctr")
    devices = lax.axis_size("pair") * ctr_count
    count = int_rows.shape[1]
    square = int_tiles[0].reshape(count, TILE, TILE).transpose(1, 0, 2).reshape(TILE, count * TILE)
    spare = -(-(count * TILE) // LANES) * LANES - count * TILE
    int_names = jnp.concatenate([int_rows, int_cols], axis=0) % KT
    int_labels = jnp.pad(int_names.astype(jnp.bfloat16), ((0, TILE - 2), (0, spare - count)))
    piece = jnp.concatenate([square, int_labels], axis=1)
    gathered = lax.all_gather(piece, "pair", axis=0, tiled=True)
    target = amp_rows // VT * ctr_count + amp_cols // KT
    everyone = ("pair", "ctr")
    packed = pack(target, amp_cols % KT, amp_rows % VT, amp_tiles, devices)
    arrived = [
        lax.all_to_all(outgoing, everyone, split_axis=0, concat_axis=0, tiled=True) for outgoing in packed
    ]
    ctr = lax.axis_index("ctr").astype(jnp.int32).reshape(1)
    names = gathered.reshape(-1, TILE, piece.shape[1])[:, :2, count * TILE : count * TILE + count]
    integrals = place_integrals(names.astype(jnp.int32), gathered)
    arrived[0], integrals = lax.optimization_barrier((arrived[0], integrals))
    parts = []
    for n, quads in enumerate(QUADS):
        if n < len(QUADS) - 1:
            [value] = product(ctr, arrived[0], arrived[n], quads, integrals, 1, ctr_count // 2)
            parts.append(lax.psum_scatter(value, "ctr", scatter_dimension=0, tiled=True))
        else:
            both = swap_cores(
                *product(ctr, arrived[0], arrived[n], quads, integrals, 2, ctr_count // 2), ctr_count
            )
            parts.append(sum_depths(both, ctr_count))
    parts = [part.reshape(3, quads * 4, -1) for part, quads in zip(parts, QUADS)]
    return jnp.concatenate(parts, axis=1).reshape(144, -1)


def solution(mesh):
    placed = (
        P(("pair", "ctr"), None),
        P(("pair", "ctr")),
        P(("pair", "ctr")),
        P("ctr", "pair", None),
        P("ctr", "pair"),
        P("ctr", "pair"),
    )
    return jax.shard_map(
        on_device, mesh=mesh, in_specs=placed, out_specs=P(("pair", "ctr"), None), check_vma=False
    )
```
